32 devices in a mesh: rows: 8 (over z, y), aux: 4 (over x, core).
Axes of the slice: x: 2, y: 2, z: 4, core: 2. Of those that a mesh axis runs over, the one named last changes fastest.
Arguments:
- density: bfloat16 [128, 8, 4096], P('aux', None, 'rows'), may hold values from -64 to 64, as said below
- vir_coeffs: bfloat16 [4096, 4096], P('rows'), may hold values from -0.09375 to 0.09375
- occ_coeffs: bfloat16 [8, 4096], P(None, 'rows'), may hold values from -2 to 2
- shell_len: int32 [8, 64], replicated, may hold values from 1 to 16, 512 in all within a row
- mu_shell: int32 [2048], P('rows'), may hold values from 0 to 511
- nu_shell: int32 [2048], P('rows'), may hold values from 0 to 63
- owner: int32 [2048, 1], P('rows'), may hold values from 0 to 7; in each aligned block of 256 rows (0 to 255, 256 to 511, ...) at most 64 rows name the same one
Outputs:
- pair_blocks: bfloat16 [4096, 128, 256], P('rows', 'aux')
- pair_scale: float32 [4096], P('rows')
The draws below stay inside these ranges and needn't reach their ends.
Inputs may be any that keep to these rules, and one draw needn't show every extreme that they name: Each index of rows names at most 64 of its 256 pairs for one owner, and exactly 64 for some owner. `shell_len`: shell lengths of each slab sum to 512; the longest is 16. `density`: Real-valued, of varying scale over auxiliary functions and orbital pairs.
All inputs are finite; a program needn't handle non-finite values.
Results may differ from the reference program's by a relative error of at most 0.0049.
Values may be sent and summed in bfloat16 or wider, within the bound.
No kernel may reach another device: no remote copies, remote signals or barrier semaphores. Data moves between devices by JAX's collectives and lax.ppermute only.
A program may use at most 192 MiB of HBM per device.

```python
import math
import jax
import jax.numpy as jnp
import numpy as np
from jax import lax

O = 8
NAUX = 128
NAO_DEV = 512
SH_DEV = 64
PAD = 16
PAIRS_DEV = 256
V = 4096
NAO = 4096
NSH = 512
CAP = 64
NPAIR = 2048
SLOTS = 4096
N_ROWS = 8


def draw_density(key, part):
    key_base, key_row, key_col = jax.random.split(jax.random.fold_in(key, 17), 3)
    ramp = 3.0 ** (jnp.arange(NAUX, dtype=jnp.float32) / (NAUX - 1))
    row_scale = ramp * jnp.exp(jax.random.uniform(key_row, (NAUX,), minval=0.0, maxval=math.log(3.5)))
    col_scale = jnp.exp(jax.random.uniform(key_col, (O, V), minval=0.0, maxval=math.log(10.0)))
    base = jnp.clip(jax.random.normal(key_base, (NAUX, O, V), dtype=jnp.float32), -6.0, 6.0)
    values = 0.1 * base * row_scale[:, None, None] * col_scale[None, :, :]
    return values.astype(jnp.bfloat16)


def place_ends(array, key, least, largest):
    extent = array.shape
    spot = [jax.random.randint(jax.random.fold_in(key, axis), (), 0, extent[axis]) for axis in range(len(extent))]
    array = array.at[tuple(spot)].set(least)
    longest = extent.index(max(extent))
    spot[longest] = (spot[longest] + 1) % extent[longest]
    return array.at[tuple(spot)].set(largest)


def shard_levels(stream_key, shape, cuts, low, high):
    def one(axis_at, parts):
        draws = jax.random.uniform(jax.random.fold_in(jax.random.fold_in(stream_key, 6), axis_at), (parts,), jnp.float32, low / len(cuts), high / len(cuts))
        return jnp.repeat(jnp.exp(draws), shape[axis_at] // parts).reshape((-1,) + (1,) * (len(shape) - axis_at - 1))

    level = one(*cuts[0])
    for cut in cuts[1:]:
        level = level * one(*cut)
    return level


def split_up(amount, total, reach, lean):
    loads = [(1 << 20) // math.isqrt(grade ** lean) + 1 for grade in range(2, amount + 1)]
    spare, counts = total - reach - (amount - 1), [1] * (amount - 1)
    while spare > 0:
        free = [i for i in range(amount - 1) if counts[i] < reach]
        whole, remaining = sum([loads[i] for i in free]), spare
        for i in free:
            more = min(reach - counts[i], max(1, remaining * loads[i] // whole), spare)
            counts[i] = counts[i] + more
            spare = spare - more
    return np.array([reach] + counts)


def ragged_sizes(key, count, total, most, skew):
    if count == 2:
        one = jax.random.randint(key, (), max(1, total - most), min(most, total - 1) + 1)
        return jnp.stack([one, total - one])
    sizes = jnp.asarray(split_up(count, total, most, skew), jnp.int32)
    pairs = (count - 1) // 2
    giver, sink = sizes[1:1 + 2 * pairs:2], sizes[2:2 + 2 * pairs:2]
    slack = jnp.minimum(giver - 1, most - sink)
    passed = jax.random.randint(jax.random.fold_in(key, 1), (pairs,), 0, 1 << 20) % (slack + 1)
    sizes = sizes.at[1:1 + 2 * pairs:2].set(giver - passed).at[2:2 + 2 * pairs:2].set(sink + passed)
    return sizes[jax.random.permutation(jax.random.fold_in(key, 2), count)]


def assign_block(stream_key, own, number, rows, count, top, limit, lean):
    sequence = jax.random.permutation(stream_key, count)
    crowded, usual = load_shares(count, rows * top, limit, lean, True), load_shares(count, rows * top, limit, lean, False)
    places = jnp.arange(count)

    def named(lengths, turn):
        used = int((lengths > 0).sum())
        fixed = max(1, used // 4)
        moved = fixed + (places - fixed + turn * (used - fixed)) % max(1, count - fixed)
        return jnp.zeros((count,), jnp.int32).at[sequence[jnp.where(places < fixed, places, moved)]].set(jnp.asarray(lengths, jnp.int32))

    lengths = jnp.where(number % 4 == 0, named(crowded, number // 4), named(usual, number - number // 4 - 1))
    mixed = jax.random.permutation(jax.random.fold_in(own, 3), count)
    giver, sink = mixed[0:count // 2 * 2:2], mixed[1:count // 2 * 2:2]
    margin = jnp.minimum(lengths[giver] - 1, limit - lengths[sink]) // 2
    margin = jnp.where((giver == sequence[0]) | (sink == sequence[0]) | (lengths[sink] == 0), 0, jnp.maximum(margin, 0))
    moved = jax.random.randint(jax.random.fold_in(own, 4), (count // 2,), 0, 1 << 20) % (margin + 1)
    lengths = lengths.at[giver].add(-moved).at[sink].add(moved)
    members = jnp.searchsorted(jnp.cumsum(lengths), jnp.arange(rows * top), side="right").astype(jnp.int32)
    listing = members.reshape(top, rows).T
    listing = listing[jax.random.permutation(jax.random.fold_in(own, 1), rows)]
    turn = jax.random.randint(jax.random.fold_in(own, 2), (rows, 1), 0, top)
    return jnp.take_along_axis(listing, (jnp.arange(top)[None, :] + turn) % top, axis=1)


def load_shares(count, total, most, slope, full):
    loads = [(1 << 20) // math.isqrt(standing ** slope) + 1 for standing in range(1, count + 1)]
    largest = most if full else min(most, max(-(-total // count), total * loads[0] // sum(loads)))
    least = 1 if total - largest >= count - 1 else 0
    holding, surplus = [largest] + [least] * (count - 1), total - largest - least * (count - 1)
    while surplus > 0:
        movable = [i for i in range(1, count) if holding[i] < largest] or [i for i in range(1, count) if holding[i] < most]
        pool, left = sum([loads[i] for i in movable]), surplus
        for i in movable:
            extra = min(most - holding[i], max(1, left * loads[i] // pool), surplus)
            holding[i] = holding[i] + extra
            surplus = surplus - extra
    return np.array(holding)


def gaussian(own_key, dims, spread, limit, cuts=(), kind=jnp.bfloat16):
    values = jax.random.normal(own_key, dims, jnp.float32) * spread
    if len(cuts) > 0:
        values = shard_levels(own_key, dims, cuts, -0.22, 0.18) * values
    return jnp.clip(values, min=-limit, max=limit).astype(kind)


def setup_inputs(seed: int = 0) -> dict:
    key_of = jax.random.split(jax.random.key(seed), 8)
    density = draw_density(jax.random.fold_in(key_of[7], 71), 0)
    vir_coeffs = gaussian(key_of[1], (NAO, V), V ** -0.5, 0.09375, ((0, 8),))
    occ_coeffs = gaussian(key_of[2], (O, NAO), O ** -0.5, 2.0, ((1, 8),))
    shell_len = jax.vmap(lambda own: ragged_sizes(own, SH_DEV, NAO_DEV, PAD, 2))(jax.random.split(key_of[3], N_ROWS)).reshape((N_ROWS, SH_DEV)).astype(jnp.int32)
    mu_shell = place_ends(jax.random.randint(key_of[4], (NPAIR,), 0, NSH), jax.random.fold_in(key_of[4], 1), 0, NSH - 1).astype(jnp.int32)
    nu_shell = place_ends(jax.random.randint(key_of[5], (NPAIR,), 0, SH_DEV), jax.random.fold_in(key_of[5], 1), 0, SH_DEV - 1).astype(jnp.int32)
    owner_keys = jax.random.split(jax.random.fold_in(key_of[6], 1), NPAIR // PAIRS_DEV)
    owner_turns = jax.random.permutation(jax.random.fold_in(key_of[6], 3), NPAIR // PAIRS_DEV)
    owner = jax.vmap(lambda own, number: assign_block(jax.random.fold_in(key_of[6], 2), own, number, PAIRS_DEV, N_ROWS, 1, CAP, 2))(owner_keys, owner_turns).reshape((NPAIR, 1))
    return dict(density=density, vir_coeffs=vir_coeffs, occ_coeffs=occ_coeffs, shell_len=shell_len, mu_shell=mu_shell, nu_shell=nu_shell, owner=owner)


def lookup(table, index):
    hits = index[:, None] == jnp.arange(table.shape[0], dtype=jnp.int32)[None, :]
    return lax.optimization_barrier(jnp.sum(jnp.where(hits, table[None, :], 0), axis=1)).astype(jnp.int32)

def reference(density, vir_coeffs, occ_coeffs, shell_len, mu_shell, nu_shell, owner):
    flat = density.reshape(NAUX * O, V)
    half = jnp.dot(flat, vir_coeffs.T, preferred_element_type=jnp.float32).astype(jnp.bfloat16).reshape(NAUX, O, NAO)
    starts = jnp.cumsum(shell_len, axis=1) - shell_len
    flat_start = (starts + jnp.arange(N_ROWS, dtype=jnp.int32)[:, None] * NAO_DEV).reshape(-1).astype(jnp.int32)
    flat_len = shell_len.reshape(-1).astype(jnp.int32)
    source = jnp.arange(NPAIR, dtype=jnp.int32) // PAIRS_DEV
    mu_start = lookup(flat_start, mu_shell)
    mu_len = lookup(flat_len, mu_shell)
    nu_global = (source * SH_DEV + nu_shell).astype(jnp.int32)
    nu_start = lookup(flat_start, nu_global)
    nu_len = lookup(flat_len, nu_global)
    dest = owner[:, 0]
    onehot = (dest[:, None] == jnp.arange(N_ROWS, dtype=jnp.int32)[None, :]).astype(jnp.int32)
    onehot = onehot.reshape(N_ROWS, PAIRS_DEV, N_ROWS)
    earlier = jnp.cumsum(onehot, axis=1) - onehot
    rank = lax.optimization_barrier(jnp.sum(earlier * onehot, axis=2)).reshape(-1)
    slot = (dest * (N_ROWS * CAP) + source * CAP + rank).astype(jnp.int32)
    half_pad = jnp.pad(half, ((0, 0), (0, 0), (0, PAD)))
    occ_pad = jnp.pad(occ_coeffs, ((0, 0), (0, PAD)))
    offsets = jnp.arange(PAD, dtype=jnp.int32)

    def one_source(packed):
        mu_first, mu_count, nu_first, nu_count = packed
        h_tiles = jax.vmap(lambda start: lax.dynamic_slice_in_dim(half_pad, start, PAD, 2))(nu_first)
        h_tiles = jnp.where((offsets[None, :] < nu_count[:, None])[:, None, None, :], h_tiles, 0)
        c_tiles = jax.vmap(lambda start: lax.dynamic_slice_in_dim(occ_pad, start, PAD, 1))(mu_first)
        c_tiles = jnp.where((offsets[None, :] < mu_count[:, None])[:, None, :], c_tiles, 0)
        blocks = jnp.einsum('kim,kpin->kpmn', c_tiles.astype(jnp.float32), h_tiles.astype(jnp.float32))
        blocks = blocks.astype(jnp.bfloat16).reshape(PAIRS_DEV, NAUX, PAD * PAD)
        squares = lax.optimization_barrier(jnp.sum(jnp.square(blocks.astype(jnp.float32)), axis=(1, 2)))
        return (blocks, squares)
    packed = (mu_start.reshape(N_ROWS, PAIRS_DEV), mu_len.reshape(N_ROWS, PAIRS_DEV), nu_start.reshape(N_ROWS, PAIRS_DEV), nu_len.reshape(N_ROWS, PAIRS_DEV))
    blocks, squares = lax.map(one_source, packed)
    blocks = blocks.reshape(NPAIR, NAUX, PAD * PAD)
    squares = squares.reshape(NPAIR)
    pair_blocks = jnp.zeros((SLOTS, NAUX, PAD * PAD), jnp.bfloat16).at[slot].set(blocks)
    total = jnp.zeros((SLOTS,), jnp.float32).at[slot].set(squares)
    pair_scale = jnp.sqrt(total / (NAUX * PAD * PAD) + 1e-06)
    return (pair_blocks, pair_scale)
```

```python
import functools

import jax
import jax.numpy as jnp
from jax import lax
from jax.experimental import pallas as pl
from jax.experimental.pallas import tpu as pltpu
from jax.sharding import PartitionSpec as P

NAUX = 128
PAD = 16
LANES = 128
DIGIT = 128
GROUP = 4
STEP = 16
MIB = 1 << 20


def swap(x, k, count):
    return lax.ppermute(x, "rows", [(i, i ^ k) for i in range(count)])


def gather(x, count):
    parts = [None] * count
    parts[0] = x
    for k in range(2, count, 2):
        parts[k] = swap(x, k, count)
    for k in range(0, count, 2):
        parts[k + 1] = swap(parts[k], 1, count)
    return parts


def dot(a, b):
    return jnp.dot(a, b, preferred_element_type=jnp.float32)


def dot_t(a, b):
    return lax.dot_general(a, b, (((1,), (1,)), ((), ())), preferred_element_type=jnp.float32)


def half_kernel(count, aux, occupied, where_ref, *refs):
    parts, (vir_ref, spread_ref, out_ref, acc_ref) = refs[:count], refs[count:]
    tiles = acc_ref.shape[0]
    width = parts[0].shape[2]
    rows = aux * occupied
    total = None
    for k in range(count):
        start = pl.multiple_of((where_ref[0] ^ k) * width, width)
        block = parts[k][:aux].reshape(rows, width)
        term = dot_t(block, vir_ref[:, pl.ds(start, width)])
        total = term if total is None else total + term
    for t in range(tiles):
        acc_ref[t] = total[:, t * LANES : (t + 1) * LANES]
    columns = []
    for i in range(occupied):
        h = [acc_ref[t, pl.ds(i, aux, stride=occupied), :].astype(jnp.bfloat16) for t in range(tiles)]
        columns.append(jnp.concatenate(h, axis=0))
    mixed = dot(jnp.concatenate(columns, axis=1), spread_ref[...]).astype(jnp.bfloat16)
    wide = occupied * LANES
    for t in range(tiles):
        out_ref[:, t * wide : (t + 1) * wide] = mixed[t * aux : (t + 1) * aux]


def make_half(position, parts, vir, spread, aux, occupied):
    count = len(parts)
    slab = vir.shape[0]
    vmem = pl.BlockSpec(memory_space=pltpu.VMEM)
    return pl.pallas_call(
        functools.partial(half_kernel, count, aux, occupied),
        out_shape=jax.ShapeDtypeStruct((aux, slab * occupied), jnp.bfloat16),
        grid_spec=pltpu.PrefetchScalarGridSpec(
            num_scalar_prefetch=1,
            grid=(),
            in_specs=[vmem] * (count + 2),
            out_specs=vmem,
            scratch_shapes=[pltpu.VMEM((slab // LANES, aux * occupied, LANES), jnp.float32)],
        ),
        compiler_params=pltpu.CompilerParams(vmem_limit_bytes=44 * MIB),
    )(position, *parts, vir, spread)


def coeff_kernel(count, slots, where_ref, mu_ref, nu_ref, *refs):
    parts, (repeat_ref, out_ref, table_ref) = refs[:count], refs[count:]
    occupied, width = parts[0].shape[1:]
    tiles = width // LANES
    per_tile = PAD
    for k in range(count):
        first = (where_ref[0] ^ k) * (tiles * per_tile)
        occ = jnp.concatenate([parts[k][0, :, t * LANES : (t + 1) * LANES] for t in range(tiles)], axis=0)
        wide = dot(occ, repeat_ref[...])
        for t in range(tiles):
            for q in range(per_tile):
                table_ref[first + t * per_tile + q] = wide[
                    t * occupied : (t + 1) * occupied, q * LANES : (q + 1) * LANES
                ]
    last = count * tiles * per_tile
    table_ref[last] = jnp.zeros((occupied, LANES), jnp.float32)
    table_ref[last + 1] = jnp.zeros((occupied, LANES), jnp.float32)
    lane = lax.broadcasted_iota(jnp.int32, (occupied, LANES), 1)

    def body(s, carry):
        mu, nu = mu_ref[s], nu_ref[s]
        mu_start, mu_length, nu_length = mu // 32, mu % 32, nu % 32
        tile = mu_start // 8
        shift = (mu_start % 8) * PAD
        back = (LANES - shift) % LANES
        x = [pltpu.roll(table_ref[tile + q], back, 1) for q in range(3)]
        keep = lane < LANES - shift
        valid = lane % PAD < nu_length
        for q in range(2):
            value = jnp.where(keep, x[q], x[q + 1])
            live = valid & (lane + q * LANES < mu_length * PAD)
            out_ref[s, :, q * LANES : (q + 1) * LANES] = jnp.where(live, value, 0.0)
        return carry

    lax.fori_loop(0, slots, body, 0, unroll=4)


def make_coeffs(position, mu, nu, parts, repeat, aux):
    count = len(parts)
    _, occupied, width = parts[0].shape
    slots = mu.shape[0]
    return pl.pallas_call(
        functools.partial(coeff_kernel, count, slots),
        out_shape=jax.ShapeDtypeStruct((slots, occupied, PAD * PAD), jnp.float32),
        grid_spec=pltpu.PrefetchScalarGridSpec(
            num_scalar_prefetch=3,
            grid=(1,),
            in_specs=[pl.BlockSpec((1, occupied, width), lambda g, *_: (aux, 0, 0))] * count
            + [pl.BlockSpec(repeat.shape, lambda g, *_: (0, 0))],
            out_specs=pl.BlockSpec((slots, occupied, PAD * PAD), lambda g, *_: (0, 0, 0)),
            scratch_shapes=[pltpu.VMEM((count * width // 8 + 2, occupied, LANES), jnp.float32)],
        ),
        compiler_params=pltpu.CompilerParams(vmem_limit_bytes=44 * MIB),
    )(position, mu, nu, *parts, repeat)


def block_kernel(base, step, where_ref, nu_ref, live_ref, half_ref, coeff_ref, *refs):
    out_ref, square_ref = refs[-2:]
    aux = half_ref.shape[0]
    occupied = coeff_ref.shape[1]
    tile_count = half_ref.shape[1] // LANES
    row = lax.broadcasted_iota(jnp.int32, (2 * PAD, PAD * PAD), 0)
    delta = row - lax.broadcasted_iota(jnp.int32, (2 * PAD, PAD * PAD), 1) % PAD
    first = pl.program_id(0) * step

    @pl.loop(0, step // GROUP)
    def _(group):
        at = group * GROUP

        @pl.when(first + at < live_ref[base])
        def _():
            for s in range(GROUP):
                nu_start = nu_ref[base, first + at + s] // 32
                tile = jnp.minimum(nu_start // PAD, tile_count - 2)
                left = half_ref[:, pl.ds(pl.multiple_of(tile * LANES, LANES), 2 * LANES)]
                hit = delta == nu_start - tile * PAD
                coeff = coeff_ref[at + s]
                rows = [jnp.where(hit, coeff[i : i + 1], 0.0).astype(jnp.bfloat16) for i in range(occupied)]
                right = jnp.concatenate([r[t * PAD : (t + 1) * PAD] for t in range(2) for r in rows], axis=0)
                block = dot(left, right).astype(jnp.bfloat16)
                out_ref[at + s] = block
                wide = block.astype(jnp.float32)
                total = jnp.sum(wide * wide, axis=0, keepdims=True)
                square_ref[pl.ds(at + s, 1), :] = total[:, :LANES] + total[:, LANES:]

        @pl.when(first + at >= live_ref[base])
        def _():
            out_ref[pl.ds(at, GROUP)] = jnp.zeros((GROUP, aux, PAD * PAD), jnp.bfloat16)
            square_ref[pl.ds(at, GROUP), :] = jnp.zeros((GROUP, LANES), jnp.float32)


def make_blocks(k, position, nu, live, half, coeffs, done, slots):
    capacity = nu.shape[1]
    aux = half.shape[0]
    occupied = coeffs.shape[1]
    step = min(STEP, capacity)
    per = capacity // step
    out_shape = (
        jax.ShapeDtypeStruct((slots, aux, PAD * PAD), jnp.bfloat16),
        jax.ShapeDtypeStruct((slots, LANES), jnp.float32),
    )
    out_specs = (
        pl.BlockSpec((step, aux, PAD * PAD), lambda g, w, n, c: ((w[0] ^ k) * per + g, 0, 0)),
        pl.BlockSpec((step, LANES), lambda g, w, n, c: ((w[0] ^ k) * per + g, 0)),
    )
    carried = [] if done is None else list(done)
    return pl.pallas_call(
        functools.partial(block_kernel, k, step),
        out_shape=out_shape,
        grid_spec=pltpu.PrefetchScalarGridSpec(
            num_scalar_prefetch=3,
            grid=(per,),
            in_specs=[
                pl.BlockSpec(half.shape, lambda g, *_: (0, 0)),
                pl.BlockSpec((step, occupied, PAD * PAD), lambda g, *_: (k * per + g, 0, 0)),
            ]
            + [pl.BlockSpec(memory_space=pl.ANY)] * len(carried),
            out_specs=out_specs,
        ),
        input_output_aliases={5 + n: n for n in range(len(carried))},
        compiler_params=pltpu.CompilerParams(vmem_limit_bytes=24 * MIB),
    )(position, nu, live, half, coeffs, *carried)


def per_device(density, vir_coeffs, occ_coeffs, shell_len, mu_shell, nu_shell, owner):
    count = lax.axis_size("rows")
    place = lax.axis_index("rows").astype(jnp.int32)
    position = place.reshape(1)
    aux, occupied, width = density.shape
    slab = vir_coeffs.shape[0]
    shells = shell_len.shape[1]
    pairs = mu_shell.shape[0]
    capacity = 2 * pairs // count
    slots = count * capacity

    digits = jnp.concatenate([mu_shell // DIGIT, mu_shell % DIGIT, nu_shell, owner[:, 0]])
    room = -(-digits.shape[0] // (occupied * width)) * occupied * width
    digits = jnp.pad(digits, (0, room - digits.shape[0])).reshape(-1, occupied, width)
    packed = jnp.concatenate([density, occ_coeffs[None], digits.astype(jnp.bfloat16)], axis=0)
    parts = gather(packed, count)

    span = occupied * LANES
    source = jnp.arange(span, dtype=jnp.int32)[:, None]
    target = jnp.arange(span, dtype=jnp.int32)[None, :]
    nu_of = source % LANES
    spread = (target == nu_of // PAD * LANES + source // LANES * PAD + nu_of % PAD).astype(jnp.bfloat16)
    repeat = (
        jnp.arange(LANES, dtype=jnp.int32)[:, None] == jnp.arange(LANES * PAD, dtype=jnp.int32)[None, :] // PAD
    ).astype(jnp.bfloat16)

    half = make_half(position, parts, vir_coeffs, spread, aux, occupied)
    halves = gather(half, count)

    got = jnp.stack([part[aux + 1 :].reshape(-1)[: 4 * pairs] for part in parts]).astype(jnp.int32)
    got = got.reshape(count, 4, pairs)
    mu, nu, wanted = got[:, 0] * DIGIT + got[:, 1], got[:, 2], got[:, 3]
    earlier = jnp.arange(shells)[:, None] < jnp.arange(shells)[None, :]
    starts = jnp.sum(jnp.where(earlier[None], shell_len[:, :, None], 0), axis=1)
    code = starts * 32 + shell_len
    mu_code = (code + jnp.arange(count, dtype=jnp.int32)[:, None] * (slab * 32)).reshape(-1)
    numbers = jnp.arange(count * shells, dtype=jnp.int32)
    sources = jnp.arange(count, dtype=jnp.int32) ^ place
    mu_found = jnp.sum(jnp.where(mu[:, :, None] == numbers, mu_code, 0), axis=2)
    nu_global = nu + sources[:, None] * shells
    nu_found = jnp.sum(jnp.where(nu_global[:, :, None] == numbers, code.reshape(-1), 0), axis=2)
    mine = wanted == place
    before = jnp.arange(pairs)[:, None] < jnp.arange(pairs)[None, :]
    rank = jnp.sum(jnp.where(before[None] & mine[:, :, None], 1, 0), axis=1)
    placed = mine[:, None, :] & (rank[:, None, :] == jnp.arange(capacity, dtype=jnp.int32)[None, :, None])
    mu_slot = jnp.sum(jnp.where(placed, mu_found[:, None, :], 0), axis=2)
    nu_slot = jnp.sum(jnp.where(placed, nu_found[:, None, :], 0), axis=2)
    live = jnp.sum(mine.astype(jnp.int32), axis=1)

    coeffs = make_coeffs(position, mu_slot.reshape(-1), nu_slot.reshape(-1), parts, repeat, aux)
    done = None
    for k in [*range(0, count, 2), *range(1, count, 2)]:
        done = make_blocks(k, position, nu_slot, live, halves[k], coeffs, done, slots)
    blocks, squares = done
    total = lax.psum(jnp.sum(squares, axis=1), "aux")
    pair_scale = jnp.sqrt(total / (NAUX * PAD * PAD) + 1e-06)
    return blocks, pair_scale


def solution(mesh):
    return jax.shard_map(
        per_device,
        mesh=mesh,
        in_specs=(
            P("aux", None, "rows"),
            P("rows", None),
            P(None, "rows"),
            P(),
            P("rows"),
            P("rows"),
            P("rows", None),
        ),
        out_specs=(P("rows", "aux", None), P("rows")),
        check_vma=False,
    )
```

```python
import functools

import jax
import jax.numpy as jnp
from jax import lax
from jax.experimental import pallas as pl
from jax.experimental.pallas import tpu as pltpu
from jax.sharding import PartitionSpec as P

NAUX = 128
PAD = 16
LANES = 128
DIGIT = 128
CODE = 32
GROUP = 16
MIB = 1 << 20
VMEM = pl.BlockSpec(memory_space=pltpu.VMEM)
HBM = pl.BlockSpec(memory_space=pltpu.HBM)


def swap(x, k, count, axis="rows"):
    return lax.ppermute(x, axis, [(i, i ^ k) for i in range(count)])


def after(x, *earlier):
    return lax.optimization_barrier((x, *earlier))[0]


def gather(x, count, first, second):
    parts = {0: x}
    for k in (4, 2):
        if k < count:
            parts[k] = swap(x, k, count)
    parts[1] = swap(x, 1, count)
    late = after(x, parts[1])
    for k in range(6, count, 2):
        parts[k] = swap(late, k, count)
    parts[3] = swap(parts[2], 1, count)
    parts[5] = swap(after(parts[4], first(parts)), 1, count)
    wait = second(parts)
    for k in range(6, count, 2):
        parts[k + 1] = swap(after(parts[k], wait) if wait is not None else parts[k], 1, count)
    return [parts[k] for k in range(count)]


def dot(a, b):
    return jnp.dot(a, b, preferred_element_type=jnp.float32)


def dot_t(a, b):
    return lax.dot_general(a, b, (((1,), (1,)), ((), ())), preferred_element_type=jnp.float32)


def whole(body, out_shape, args, scratch=(), scalars=0, specs=None, cost=None):
    outs = out_shape if isinstance(out_shape, tuple) else (out_shape,)
    return pl.pallas_call(
        body,
        out_shape=out_shape,
        grid_spec=pltpu.PrefetchScalarGridSpec(
            num_scalar_prefetch=scalars,
            grid=(),
            in_specs=specs or [VMEM] * (len(args) - scalars),
            out_specs=tuple(VMEM for _ in outs) if isinstance(out_shape, tuple) else VMEM,
            scratch_shapes=list(scratch),
        ),
        compiler_params=pltpu.CompilerParams(vmem_limit_bytes=44 * MIB),
        cost_estimate=pl.CostEstimate(flops=0, transcendentals=0, bytes_accessed=cost) if cost else None,
    )(*args)


def pack_kernel(density_ref, occ_ref, mu_ref, nu_ref, owner_ref, out_ref, small_ref, sems):
    aux, occupied, width = density_ref.shape
    pairs = mu_ref.shape[1]
    copies = [
        pltpu.make_async_copy(density_ref, out_ref.at[pl.ds(0, aux)], sems.at[0]),
        pltpu.make_async_copy(occ_ref, out_ref.at[aux], sems.at[1]),
    ]
    for n, ref in enumerate((mu_ref, nu_ref, owner_ref)):
        copies.append(pltpu.make_async_copy(ref, small_ref.at[n], sems.at[2 + n]))
    for copy in copies:
        copy.start()
    for copy in copies[2:]:
        copy.wait()
    mu = small_ref[0]
    digits = [mu // DIGIT, mu % DIGIT, small_ref[1], small_ref[2]]
    per = width // pairs
    rows = [jnp.concatenate(digits[n : n + per], axis=1) for n in range(0, 4, per)]
    rows.append(jnp.zeros((occupied - len(rows), width), jnp.int32))
    out_ref[aux + 1] = jnp.concatenate(rows, axis=0).astype(jnp.float32).astype(jnp.bfloat16)
    for copy in copies[:2]:
        copy.wait()


def part_kernel(ks, resumed, ahead, aux, where_ref, vir_ref, *refs):
    refs = list(refs)
    blocks = [refs.pop(0) for _ in ks]
    before_ref = refs.pop(0) if resumed else None
    total_ref, token_ref = refs.pop(0), refs.pop(0)
    ahead_ref = refs.pop(0) if ahead is not None else None
    token_ref[...] = jnp.zeros(token_ref.shape, jnp.float32)
    columns_ref, sems = refs
    _, occupied, width = blocks[0].shape

    def fetch(k, target, n):
        start = pl.multiple_of((where_ref[0] ^ k) * width, width)
        return pltpu.make_async_copy(vir_ref.at[:, pl.ds(start, width)], target, sems.at[n])

    copies = [fetch(k, columns_ref.at[n], n) for n, k in enumerate(ks)]
    if ahead is not None:
        copies.append(fetch(ahead, ahead_ref, len(ks)))
    for copy in copies:
        copy.start()
    total = None if before_ref is None else before_ref[...]
    for n in range(len(ks)):
        copies[n].wait()
        term = dot_t(blocks[n][:aux].reshape(aux * occupied, width), columns_ref[n])
        total = term if total is None else total + term
    total_ref[...] = total
    if ahead is not None:
        copies[-1].wait()


def add_part(position, vir, parts, ks, before, ahead, aux):
    slab = vir.shape[0]
    _, occupied, width = parts[0].shape
    out = [jax.ShapeDtypeStruct(shape, jnp.float32) for shape in ((aux * occupied, slab), (8, LANES))]
    if ahead is not None:
        out.append(jax.ShapeDtypeStruct((slab, width), vir.dtype))
    args = [position, vir] + [parts[k] for k in ks] + ([] if before is None else [before])
    return whole(
        functools.partial(part_kernel, ks, before is not None, ahead, aux),
        tuple(out),
        args,
        scratch=[
            pltpu.VMEM((len(ks), slab, width), vir.dtype),
            pltpu.SemaphoreType.DMA((len(ks) + 1,)),
        ],
        scalars=1,
        specs=[HBM] + [VMEM] * (len(args) - 2),
        cost=len(ks) * 2 * MIB,
    )


def half_kernel(aux, before_ref, part_ref, column_ref, spread_ref, out_ref, total_ref):
    _, occupied, width = part_ref.shape
    tiles = total_ref.shape[0]
    total = before_ref[...] + dot_t(part_ref[:aux].reshape(aux * occupied, width), column_ref[...])
    for t in range(tiles):
        total_ref[t] = total[:, t * LANES : (t + 1) * LANES]
    columns = []
    for i in range(occupied):
        h = [total_ref[t, pl.ds(i, aux, stride=occupied), :].astype(jnp.bfloat16) for t in range(tiles)]
        columns.append(jnp.concatenate(h, axis=0))
    mixed = dot(jnp.concatenate(columns, axis=1), spread_ref[...]).astype(jnp.bfloat16)
    wide = occupied * LANES
    for t in range(tiles):
        out_ref[:, t * wide : (t + 1) * wide] = mixed[t * aux : (t + 1) * aux]


def make_half(position, packed, vir, spread, aux):
    count = lax.axis_size("rows")
    slab = vir.shape[0]
    occupied = packed.shape[1]
    order = [0, 1, 2, 4] + list(range(6, count, 2)) + list(range(3, count, 2))
    early, middle, last = order[:4], order[4:-1], order[-1]
    totals = []

    def start(parts):
        total, token = add_part(position, vir, parts, early, None, None, aux)
        totals.append(total)
        return token

    parts = gather(packed, count, start, lambda parts: None)
    total, _, column = add_part(position, vir, parts, middle, totals[0], last, aux)
    half = whole(
        functools.partial(half_kernel, aux),
        jax.ShapeDtypeStruct((aux, slab * occupied), jnp.bfloat16),
        [total, parts[last], column, spread],
        scratch=[pltpu.VMEM((slab // LANES, aux * occupied, LANES), jnp.float32)],
        cost=4 * MIB,
    )
    return half, parts


def table_kernel(count, pairs, capacity, shells, slab, where_ref, *refs):
    parts, (shell_ref, repeat_ref, meta_ref, table_ref, digit_ref) = refs[:count], refs[count:]
    occupied, width = parts[0].shape[1:]
    tiles = width // LANES
    for k in range(count):
        first = (where_ref[0] ^ k) * (tiles * PAD)
        occ = jnp.concatenate([parts[k][0, :, t * LANES : (t + 1) * LANES] for t in range(tiles)], axis=0)
        wide = dot(occ, repeat_ref[...])
        for t in range(tiles):
            for q in range(PAD):
                table_ref[first + t * PAD + q] = wide[
                    t * occupied : (t + 1) * occupied, q * LANES : (q + 1) * LANES
                ]
        digit_ref[k] = parts[k][1].astype(jnp.float32)
    last = count * tiles * PAD
    table_ref[last] = jnp.zeros((occupied, LANES), jnp.float32)
    table_ref[last + 1] = jnp.zeros((occupied, LANES), jnp.float32)
    meta_ref[2 * count :, :] = jnp.full((meta_ref.shape[0] - 2 * count, LANES), where_ref[0], jnp.int32)

    per = width // pairs
    total = shell_ref.shape[1]
    f32, bf16 = jnp.float32, jnp.bfloat16
    before = (
        lax.broadcasted_iota(jnp.int32, (pairs, pairs), 0) < lax.broadcasted_iota(jnp.int32, (pairs, pairs), 1)
    ).astype(f32).astype(bf16)
    number = lax.broadcasted_iota(jnp.int32, (total, pairs), 0).astype(f32)
    slot = lax.broadcasted_iota(jnp.int32, (LANES, pairs), 0).astype(f32)
    place = where_ref[0].astype(f32)

    def body(k, carry):
        source = (where_ref[0] ^ k).astype(f32)
        rows = digit_ref[k]
        d = [rows[n // per : n // per + 1, n % per * pairs : (n % per + 1) * pairs] for n in range(4)]
        mu = d[0] * DIGIT + d[1]
        nu = d[2] + source * shells
        mine = jnp.where(d[3] == place, 1.0, 0.0)
        rank = dot(jnp.broadcast_to(mine, (8, pairs)).astype(bf16), before)[:1]
        rank = jnp.where(mine > 0, rank, -1.0)
        found = []
        for wanted in (mu, nu):
            hits = jnp.where(number == wanted, 1.0, 0.0).astype(bf16)
            found.append(dot(shell_ref[...], hits).astype(bf16))
        placed = [
            jnp.where((slot == rank + shift) & (rank >= 0), 1.0, 0.0).astype(bf16) for shift in (0, capacity)
        ]
        mixed = dot_t(found[0], placed[0]) + dot_t(found[1], placed[1])
        code = ((mixed[0:1] * DIGIT + mixed[1:2]) * CODE + mixed[2:3]).astype(jnp.int32)
        meta_ref[pl.ds(k, 1), :] = code
        live = jnp.sum(mine, axis=1, keepdims=True).astype(jnp.int32)
        meta_ref[pl.ds(count + k, 1), :] = jnp.broadcast_to(live, (1, LANES))
        return carry

    lax.fori_loop(0, count, body, 0)


def make_tables(position, parts, shell_table, repeat, pairs, capacity, shells, slab, aux):
    count = len(parts)
    _, occupied, width = parts[0].shape
    return pl.pallas_call(
        functools.partial(table_kernel, count, pairs, capacity, shells, slab),
        out_shape=(
            jax.ShapeDtypeStruct((2 * count + 8, LANES), jnp.int32),
            jax.ShapeDtypeStruct((count * width // 8 + 2, occupied, LANES), jnp.float32),
        ),
        grid_spec=pltpu.PrefetchScalarGridSpec(
            num_scalar_prefetch=1,
            grid=(1,),
            in_specs=[pl.BlockSpec((2, occupied, width), lambda g, w: (aux // 2, 0, 0))] * count + [VMEM] * 2,
            out_specs=(VMEM, VMEM),
            scratch_shapes=[pltpu.VMEM((count, occupied, width), jnp.float32)],
        ),
        compiler_params=pltpu.CompilerParams(vmem_limit_bytes=44 * MIB),
        cost_estimate=pl.CostEstimate(flops=0, transcendentals=0, bytes_accessed=16 * MIB),
    )(position, *parts, shell_table, repeat)


def window(ref, tile, shift, lane):
    top = ref.shape[1] // LANES - 1
    tiles = [ref[:, pl.ds(pl.multiple_of(t * LANES, LANES), LANES)] for t in (tile, jnp.minimum(tile + 1, top))]
    turned = [pltpu.roll(t.astype(jnp.float32), (LANES - shift) % LANES, 1) for t in tiles]
    return jnp.where(lane < LANES - shift, turned[0], turned[1]).astype(jnp.bfloat16)


def block_kernel(ks, resumed, group, count, capacity, slab, meta_ref, table_ref, *refs):
    refs = list(refs)
    halves = [refs.pop(0) for _ in ks]
    old_sum_ref = refs.pop(1) if resumed else None
    if resumed:
        refs.pop(0)
    out_ref, sum_ref, buffer_ref, zero_ref, square_ref, sems = refs
    aux = halves[0].shape[0]
    occupied = table_ref.shape[1]
    per = LANES // occupied
    lane = lax.broadcasted_iota(jnp.int32, (occupied, LANES), 1)
    column = lane % PAD
    wide_lane = lax.broadcasted_iota(jnp.int32, (aux, LANES), 1)
    ones = jnp.ones((8, LANES), jnp.float32)
    zero_ref[...] = jnp.zeros(zero_ref.shape, zero_ref.dtype)
    sum_ref[...] = old_sum_ref[...] if resumed else jnp.zeros(sum_ref.shape, jnp.float32)
    groups = capacity // group

    for n, k in enumerate(ks):
        base = meta_ref[2 * count, 0] ^ k
        live = meta_ref[count + k, 0]

        def send(source, at, n=n, base=base):
            target = out_ref.at[pl.ds(base * capacity + at, group)]
            return pltpu.make_async_copy(source, target, sems.at[n * groups + at // group])

        @pl.loop(0, groups)
        def _(turn, n=n, k=k, base=base, live=live, send=send):
            at = turn * group

            @pl.when(at < live)
            def _():
                for s in range(group):
                    mu, nu = meta_ref[k, at + s], meta_ref[k, capacity + at + s]
                    mu_start, mu_length = mu // CODE, mu % CODE
                    nu_length = nu % CODE
                    nu_start = jnp.maximum(nu // CODE - base * slab, 0)
                    left = window(halves[n], nu_start // per, nu_start % per * occupied, wide_lane)
                    tile, shift = mu_start // (LANES // PAD), mu_start % (LANES // PAD) * PAD
                    x = [pltpu.roll(table_ref[tile + q], (LANES - shift) % LANES, 1) for q in range(3)]
                    keep = lane < LANES - shift
                    coeff = []
                    for q in range(2):
                        valid = (column < nu_length) & (lane + q * LANES < mu_length * PAD)
                        coeff.append(jnp.where(valid, jnp.where(keep, x[q], x[q + 1]), 0.0))
                    right = [
                        jnp.concatenate([jnp.where(column == m, c, 0.0) for m in range(PAD)], axis=0) for c in coeff
                    ]
                    right = jnp.concatenate(right, axis=1).astype(jnp.bfloat16)
                    block = dot(left, right).astype(jnp.bfloat16)
                    buffer_ref[n, at + s] = block
                    wide = block.astype(jnp.float32)
                    total = jnp.sum(wide * wide, axis=0, keepdims=True)
                    square_ref[pl.ds(at + s, 1), :] = total[:, :LANES] + total[:, LANES:]
                send(buffer_ref.at[n, pl.ds(at, group)], at).start()

            @pl.when(at >= live)
            def _():
                square_ref[pl.ds(at, group), :] = jnp.zeros((group, LANES), jnp.float32)
                send(zero_ref, at).start()

        sums = lax.dot_general(
            ones,
            square_ref[...],
            (((1,), (1,)), ((), ())),
            precision=lax.Precision.HIGHEST,
            preferred_element_type=jnp.float32,
        )
        sum_ref[pl.ds(base, 1), :] = sums[:1]

    for n, k in enumerate(ks):
        base = meta_ref[2 * count, 0] ^ k
        for turn in range(groups):
            target = out_ref.at[pl.ds(base * capacity + turn * group, group)]
            pltpu.make_async_copy(zero_ref, target, sems.at[n * groups + turn]).wait()


def make_blocks(ks, count, capacity, slab, meta, halves, table, done):
    aux = halves[ks[0]].shape[0]
    slots = count * capacity
    group = min(GROUP, capacity)
    carried = [] if done is None else list(done)
    return pl.pallas_call(
        functools.partial(block_kernel, ks, bool(carried), group, count, capacity, slab),
        out_shape=(
            jax.ShapeDtypeStruct((slots, aux, PAD * PAD), jnp.bfloat16),
            jax.ShapeDtypeStruct((count, capacity), jnp.float32),
        ),
        grid_spec=pltpu.PrefetchScalarGridSpec(
            num_scalar_prefetch=1,
            grid=(),
            in_specs=[VMEM] * (1 + len(ks)) + ([HBM, VMEM] if carried else []),
            out_specs=(HBM, VMEM),
            scratch_shapes=[
                pltpu.VMEM((len(ks), capacity, aux, PAD * PAD), jnp.bfloat16),
                pltpu.VMEM((group, aux, PAD * PAD), jnp.bfloat16),
                pltpu.VMEM((capacity, LANES), jnp.float32),
                pltpu.SemaphoreType.DMA((len(ks) * capacity // group,)),
            ],
        ),
        input_output_aliases={2 + len(ks): 0} if carried else {},
        compiler_params=pltpu.CompilerParams(vmem_limit_bytes=24 * MIB),
        cost_estimate=pl.CostEstimate(flops=0, transcendentals=0, bytes_accessed=len(ks) * 6 * MIB),
    )(meta, table, *[halves[k] for k in ks], *carried)


def per_device(density, vir_coeffs, occ_coeffs, shell_len, mu_shell, nu_shell, owner):
    count = lax.axis_size("rows")
    columns = lax.axis_size("aux")
    position = lax.axis_index("rows").astype(jnp.int32).reshape(1)
    aux, occupied, width = density.shape
    slab = vir_coeffs.shape[0]
    shells = shell_len.shape[1]
    pairs = mu_shell.shape[0]
    capacity = 2 * pairs // count

    packed = whole(
        pack_kernel,
        jax.ShapeDtypeStruct((aux + 2, occupied, width), jnp.bfloat16),
        [density, occ_coeffs, mu_shell.reshape(1, pairs), nu_shell.reshape(1, pairs), owner.reshape(1, pairs)],
        scratch=[pltpu.VMEM((3, 1, pairs), jnp.int32), pltpu.SemaphoreType.DMA((5,))],
        specs=[HBM] * 5,
    )

    span = occupied * LANES
    source = jnp.arange(span, dtype=jnp.int32)[:, None]
    target = jnp.arange(span, dtype=jnp.int32)[None, :]
    spread = (target == source % LANES * occupied + source // LANES).astype(jnp.bfloat16)
    repeat = (
        jnp.arange(LANES, dtype=jnp.int32)[:, None] == jnp.arange(LANES * PAD, dtype=jnp.int32)[None, :] // PAD
    ).astype(jnp.bfloat16)
    earlier = jnp.arange(shells)[:, None] < jnp.arange(shells)[None, :]
    starts = jnp.sum(jnp.where(earlier[None], shell_len[:, :, None], 0), axis=1)
    starts = (starts + jnp.arange(count, dtype=jnp.int32)[:, None] * slab).reshape(-1)
    digits = jnp.stack([starts // DIGIT, starts % DIGIT, shell_len.reshape(-1)])
    shell_table = jnp.pad(digits, ((0, 5), (0, 0))).astype(jnp.bfloat16)

    half, parts = make_half(position, packed, vir_coeffs, spread, aux)
    state = {}

    def tables(halves):
        state["meta"], state["table"] = make_tables(
            position, parts, shell_table, repeat, pairs, capacity, shells, slab, aux
        )
        return state["meta"]

    def blocks_of(ks, halves):
        state["done"] = make_blocks(
            ks, count, capacity, slab, state["meta"], halves, state["table"], state.get("done")
        )
        return state["done"][1]

    halves = gather(half, count, tables, lambda halves: blocks_of([0, 1, 2], halves))
    blocks_of([4, *range(6, count, 2), 3], halves)
    for k in range(5, count, 2):
        blocks_of([k], halves)
    blocks, sums = state["done"]
    sums = [sums] + [swap(sums, k, columns, "aux") for k in range(1, columns)]
    while len(sums) > 1:
        sums = [sums[n] + sums[n + 1] for n in range(0, len(sums), 2)]
    pair_scale = jnp.sqrt(sums[0].reshape(-1) / (NAUX * PAD * PAD) + 1e-06)
    return blocks, pair_scale


def solution(mesh):
    return jax.shard_map(
        per_device,
        mesh=mesh,
        in_specs=(
            P("aux", None, "rows"),
            P("rows", None),
            P(None, "rows"),
            P(),
            P("rows"),
            P("rows"),
            P("rows", None),
        ),
        out_specs=(P("rows", "aux", None), P("rows")),
        check_vma=False,
    )
```

```python
import functools

import jax
import jax.numpy as jnp
from jax import lax
from jax.experimental import pallas as pl
from jax.experimental.pallas import tpu as pltpu
from jax.sharding import PartitionSpec as P

NAUX = 128
PAD = 16
LANES = 128
DIGIT = 128
CODE_BITS = 5
CODE = 1 << CODE_BITS
GROUP = 32
MIB = 1 << 20
VMEM = pl.BlockSpec(memory_space=pltpu.VMEM)
HBM = pl.BlockSpec(memory_space=pltpu.HBM)


def swap(x, k, count, axis="rows"):
    return lax.ppermute(x, axis, [(i, i ^ k) for i in range(count)])


def tie(*arrays):
    return lax.optimization_barrier(arrays)


def gather(x, count, name, early):
    parts = {0: x}

    def move(k, value, by):
        with jax.named_scope(f"{name}_{k}"):
            parts[k] = swap(value, by, count)

    for k in (4, 2):
        if k < count:
            move(k, x, k)
    move(1, x, 1)
    x, parts[1] = tie(x, parts[1])
    for k in range(6, count, 2):
        move(k, x, k)
    move(3, parts[2], 1)
    parts[4], parts[3], result = tie(parts[4], parts[3], early(parts))
    for k in range(4, count, 2):
        move(k + 1, parts[k], 1)
    return [parts[k] for k in range(count)], result


def dot(a, b):
    return jnp.dot(a, b, preferred_element_type=jnp.float32)


def dot_t(a, b):
    return lax.dot_general(a, b, (((1,), (1,)), ((), ())), preferred_element_type=jnp.float32)


def whole(body, out_shape, args, scratch=(), scalars=0, specs=None, cost=None, limit=44):
    outs = out_shape if isinstance(out_shape, tuple) else (out_shape,)
    return pl.pallas_call(
        body,
        out_shape=out_shape,
        grid_spec=pltpu.PrefetchScalarGridSpec(
            num_scalar_prefetch=scalars,
            grid=(),
            in_specs=specs or [VMEM] * (len(args) - scalars),
            out_specs=tuple(VMEM for _ in outs) if isinstance(out_shape, tuple) else VMEM,
            scratch_shapes=list(scratch),
        ),
        compiler_params=pltpu.CompilerParams(vmem_limit_bytes=limit * MIB),
        cost_estimate=pl.CostEstimate(flops=0, transcendentals=0, bytes_accessed=cost) if cost else None,
    )(*args)


def pack_kernel(density_ref, occ_ref, mu_ref, nu_ref, owner_ref, out_ref, small_ref, sems):
    aux, occupied, width = density_ref.shape
    pairs = mu_ref.shape[1]
    copies = [
        pltpu.make_async_copy(density_ref, out_ref.at[pl.ds(0, aux)], sems.at[0]),
        pltpu.make_async_copy(occ_ref, out_ref.at[aux], sems.at[1]),
    ]
    for n, ref in enumerate((mu_ref, nu_ref, owner_ref)):
        copies.append(pltpu.make_async_copy(ref, small_ref.at[n], sems.at[2 + n]))
    for copy in copies:
        copy.start()
    for copy in copies[2:]:
        copy.wait()
    mu = small_ref[0]
    digits = [mu // DIGIT, mu % DIGIT, small_ref[1], small_ref[2]]
    per = width // pairs
    rows = [jnp.concatenate(digits[n : n + per], axis=1) for n in range(0, 4, per)]
    rows.append(jnp.zeros((occupied - len(rows), width), jnp.int32))
    out_ref[aux + 1] = jnp.concatenate(rows, axis=0).astype(jnp.float32).astype(jnp.bfloat16)
    for copy in copies[:2]:
        copy.wait()


def part_kernel(ks, resumed, ahead, aux, where_ref, vir_ref, *refs):
    refs = list(refs)
    blocks = [refs.pop(0) for _ in ks]
    before_ref = refs.pop(0) if resumed else None
    total_ref = refs.pop(0)
    ahead_ref = refs.pop(0) if ahead is not None else None
    columns_ref, sems = refs
    _, occupied, width = blocks[0].shape

    def fetch(k, target, n):
        start = pl.multiple_of((where_ref[0] ^ k) * width, width)
        return pltpu.make_async_copy(vir_ref.at[:, pl.ds(start, width)], target, sems.at[n])

    copies = [fetch(k, columns_ref.at[n], n) for n, k in enumerate(ks)]
    if ahead is not None:
        copies.append(fetch(ahead, ahead_ref, len(ks)))
    for copy in copies:
        copy.start()
    total = None if before_ref is None else before_ref[...]
    for n in range(len(ks)):
        copies[n].wait()
        term = dot_t(blocks[n][:aux].reshape(aux * occupied, width), columns_ref[n])
        total = term if total is None else total + term
    total_ref[...] = total
    if ahead is not None:
        copies[-1].wait()


def add_part(position, vir, parts, ks, before, ahead, aux):
    slab = vir.shape[0]
    _, occupied, width = parts[0].shape
    out = [jax.ShapeDtypeStruct((aux * occupied, slab), jnp.float32)]
    if ahead is not None:
        out.append(jax.ShapeDtypeStruct((slab, width), vir.dtype))
    args = [position, vir] + [parts[k] for k in ks] + ([] if before is None else [before])
    return whole(
        functools.partial(part_kernel, ks, before is not None, ahead, aux),
        tuple(out),
        args,
        scratch=[
            pltpu.VMEM((len(ks), slab, width), vir.dtype),
            pltpu.SemaphoreType.DMA((len(ks) + 1,)),
        ],
        scalars=1,
        specs=[HBM] + [VMEM] * (len(args) - 2),
        cost=len(ks) * 2 * MIB,
    )


def half_kernel(aux, before_ref, part_ref, column_ref, spread_ref, out_ref, total_ref):
    _, occupied, width = part_ref.shape
    tiles = total_ref.shape[0]
    total = before_ref[...] + dot_t(part_ref[:aux].reshape(aux * occupied, width), column_ref[...])
    for t in range(tiles):
        total_ref[t] = total[:, t * LANES : (t + 1) * LANES]
    columns = []
    for i in range(occupied):
        h = [total_ref[t, pl.ds(i, aux, stride=occupied), :].astype(jnp.bfloat16) for t in range(tiles)]
        columns.append(jnp.concatenate(h, axis=0))
    mixed = dot(jnp.concatenate(columns, axis=1), spread_ref[...]).astype(jnp.bfloat16)
    wide = occupied * LANES
    for t in range(tiles):
        out_ref[:, t * wide : (t + 1) * wide] = mixed[t * aux : (t + 1) * aux]


def make_half(position, packed, vir, spread, aux):
    count = lax.axis_size("rows")
    slab = vir.shape[0]
    occupied = packed.shape[1]
    order = [0, 1, 2, 3] + list(range(4, count, 2)) + list(range(5, count, 2))
    early, middle, last = order[:4], order[4:-1], order[-1]
    parts, total = gather(
        packed, count, "density", lambda parts: add_part(position, vir, parts, early, None, None, aux)[0]
    )
    total, column = add_part(position, vir, parts, middle, total, last, aux)
    half = whole(
        functools.partial(half_kernel, aux),
        jax.ShapeDtypeStruct((aux, slab * occupied), jnp.bfloat16),
        [total, parts[last], column, spread],
        scratch=[pltpu.VMEM((slab // LANES, aux * occupied, LANES), jnp.float32)],
        cost=4 * MIB,
    )
    return half, parts


def table_kernel(count, pairs, capacity, shells, slab, where_ref, *refs):
    parts, (shell_ref, repeat_ref, meta_ref, table_ref, digit_ref) = refs[:count], refs[count:]
    occupied, width = parts[0].shape[1:]
    tiles = width // LANES
    for k in range(count):
        first = (where_ref[0] ^ k) * (tiles * PAD)
        occ = jnp.concatenate([parts[k][0, :, t * LANES : (t + 1) * LANES] for t in range(tiles)], axis=0)
        wide = dot(occ, repeat_ref[...])
        for t in range(tiles):
            for q in range(PAD):
                table_ref[first + t * PAD + q] = wide[
                    t * occupied : (t + 1) * occupied, q * LANES : (q + 1) * LANES
                ]
        digit_ref[k] = parts[k][1].astype(jnp.float32)
    last = count * tiles * PAD
    table_ref[last] = jnp.zeros((occupied, LANES), jnp.float32)
    table_ref[last + 1] = jnp.zeros((occupied, LANES), jnp.float32)
    meta_ref[2 * count :, :] = jnp.full((meta_ref.shape[0] - 2 * count, LANES), where_ref[0], jnp.int32)

    per = width // pairs
    total = shell_ref.shape[1]
    f32, bf16 = jnp.float32, jnp.bfloat16
    before = (
        lax.broadcasted_iota(jnp.int32, (pairs, pairs), 0) < lax.broadcasted_iota(jnp.int32, (pairs, pairs), 1)
    ).astype(f32).astype(bf16)
    number = lax.broadcasted_iota(jnp.int32, (total, pairs), 0).astype(f32)
    slot = lax.broadcasted_iota(jnp.int32, (LANES, pairs), 0).astype(f32)
    place = where_ref[0].astype(f32)

    def body(k, carry):
        source = (where_ref[0] ^ k).astype(f32)
        rows = digit_ref[k]
        d = [rows[n // per : n // per + 1, n % per * pairs : (n % per + 1) * pairs] for n in range(4)]
        mu = d[0] * DIGIT + d[1]
        nu = d[2] + source * shells
        mine = jnp.where(d[3] == place, 1.0, 0.0)
        rank = dot(jnp.broadcast_to(mine, (8, pairs)).astype(bf16), before)[:1]
        rank = jnp.where(mine > 0, rank, -1.0)
        found = []
        for wanted in (mu, nu):
            hits = jnp.where(number == wanted, 1.0, 0.0).astype(bf16)
            found.append(dot(shell_ref[...], hits).astype(bf16))
        placed = [
            jnp.where((slot == rank + shift) & (rank >= 0), 1.0, 0.0).astype(bf16) for shift in (0, capacity)
        ]
        mixed = dot_t(found[0], placed[0]) + dot_t(found[1], placed[1])
        start = mixed[0:1] * DIGIT + mixed[1:2]
        number_of = lax.broadcasted_iota(jnp.int32, (1, LANES), 1)
        start = jnp.where(number_of < capacity, start, jnp.maximum(start - source * slab, 0.0))
        code = (start * CODE + mixed[2:3]).astype(jnp.int32)
        meta_ref[pl.ds(k, 1), :] = code
        live = jnp.sum(mine, axis=1, keepdims=True).astype(jnp.int32)
        meta_ref[pl.ds(count + k, 1), :] = jnp.broadcast_to(live, (1, LANES))
        return carry

    lax.fori_loop(0, count, body, 0)


def make_tables(position, parts, shell_table, repeat, pairs, capacity, shells, slab, aux):
    count = len(parts)
    _, occupied, width = parts[0].shape
    return pl.pallas_call(
        functools.partial(table_kernel, count, pairs, capacity, shells, slab),
        out_shape=(
            jax.ShapeDtypeStruct((2 * count + 8, LANES), jnp.int32),
            jax.ShapeDtypeStruct((count * width // 8 + 2, occupied, LANES), jnp.float32),
        ),
        grid_spec=pltpu.PrefetchScalarGridSpec(
            num_scalar_prefetch=1,
            grid=(1,),
            in_specs=[pl.BlockSpec((2, occupied, width), lambda g, w: (aux // 2, 0, 0))] * count + [VMEM] * 2,
            out_specs=(VMEM, VMEM),
            scratch_shapes=[pltpu.VMEM((count, occupied, width), jnp.float32)],
        ),
        compiler_params=pltpu.CompilerParams(vmem_limit_bytes=44 * MIB),
        cost_estimate=pl.CostEstimate(flops=0, transcendentals=0, bytes_accessed=16 * MIB),
    )(position, *parts, shell_table, repeat)


def window(ref, tile, shift, lane):
    top = ref.shape[1] // LANES - 1
    tiles = [ref[:, pl.ds(pl.multiple_of(t * LANES, LANES), LANES)] for t in (tile, jnp.minimum(tile + 1, top))]
    turned = [pltpu.roll(t.astype(jnp.float32), (LANES - shift) & (LANES - 1), 1) for t in tiles]
    return jnp.where(lane < LANES - shift, turned[0], turned[1]).astype(jnp.bfloat16)


def block_kernel(ks, resumed, group, count, capacity, slab, meta_ref, table_ref, *refs):
    refs = list(refs)
    halves = [refs.pop(0) for _ in ks]
    old_sum_ref = refs.pop(1) if resumed else None
    if resumed:
        refs.pop(0)
    out_ref, sum_ref, buffer_ref, zero_ref, square_ref, sems = refs
    aux = halves[0].shape[0]
    occupied = table_ref.shape[1]
    per = LANES // occupied
    per_bits = per.bit_length() - 1
    lane = lax.broadcasted_iota(jnp.int32, (occupied, LANES), 1)
    column = lane % PAD
    wide_lane = lax.broadcasted_iota(jnp.int32, (aux, LANES), 1)
    ones = jnp.ones((8, LANES), jnp.float32)
    zero_ref[...] = jnp.zeros(zero_ref.shape, zero_ref.dtype)
    sum_ref[...] = old_sum_ref[...] if resumed else jnp.zeros(sum_ref.shape, jnp.float32)
    groups = capacity // group

    for n, k in enumerate(ks):
        base = meta_ref[2 * count, 0] ^ k
        live = meta_ref[count + k, 0]

        def send(source, at, n=n, base=base):
            target = out_ref.at[pl.ds(base * capacity + at, group)]
            return pltpu.make_async_copy(source, target, sems.at[n * groups + at // group])

        @pl.loop(0, groups)
        def _(turn, n=n, k=k, base=base, live=live, send=send):
            at = turn * group

            @pl.when(at < live)
            def _():
                for s in range(group):
                    mu, nu = meta_ref[k, at + s], meta_ref[k, capacity + at + s]
                    mu_wide, nu_length = (mu & (CODE - 1)) * PAD, nu & (CODE - 1)
                    nu_tile, nu_shift = nu >> (CODE_BITS + per_bits), (nu >> CODE_BITS) & (per - 1)
                    left = window(halves[n], nu_tile, nu_shift * occupied, wide_lane)
                    tile, shift = mu >> (CODE_BITS + 3), ((mu >> CODE_BITS) & 7) * PAD
                    back = (LANES - shift) & (LANES - 1)
                    x = [pltpu.roll(table_ref[tile + q], back, 1) for q in range(3)]
                    keep = lane < LANES - shift
                    coeff = []
                    for q in range(2):
                        valid = (column < nu_length) & (lane + q * LANES < mu_wide)
                        coeff.append(jnp.where(valid, jnp.where(keep, x[q], x[q + 1]), 0.0))
                    right = [
                        jnp.concatenate([jnp.where(column == m, c, 0.0) for m in range(PAD)], axis=0) for c in coeff
                    ]
                    right = jnp.concatenate(right, axis=1).astype(jnp.bfloat16)
                    block = dot(left, right).astype(jnp.bfloat16)
                    buffer_ref[n, at + s] = block
                    wide = block.astype(jnp.float32)
                    total = jnp.sum(wide * wide, axis=0, keepdims=True)
                    square_ref[pl.ds(at + s, 1), :] = total[:, :LANES] + total[:, LANES:]
                send(buffer_ref.at[n, pl.ds(at, group)], at).start()

            @pl.when(at >= live)
            def _():
                square_ref[pl.ds(at, group), :] = jnp.zeros((group, LANES), jnp.float32)
                send(zero_ref, at).start()

        sums = lax.dot_general(
            ones,
            square_ref[...],
            (((1,), (1,)), ((), ())),
            precision=lax.Precision.HIGHEST,
            preferred_element_type=jnp.float32,
        )
        sum_ref[pl.ds(base, 1), :] = sums[:1]

    for n, k in enumerate(ks):
        base = meta_ref[2 * count, 0] ^ k
        for turn in range(groups):
            target = out_ref.at[pl.ds(base * capacity + turn * group, group)]
            pltpu.make_async_copy(zero_ref, target, sems.at[n * groups + turn]).wait()


def make_blocks(ks, count, capacity, slab, meta, halves, table, done):
    aux = halves[ks[0]].shape[0]
    slots = count * capacity
    group = min(GROUP, capacity)
    carried = [] if done is None else list(done)
    return pl.pallas_call(
        functools.partial(block_kernel, ks, bool(carried), group, count, capacity, slab),
        out_shape=(
            jax.ShapeDtypeStruct((slots, aux, PAD * PAD), jnp.bfloat16),
            jax.ShapeDtypeStruct((count, capacity), jnp.float32),
        ),
        grid_spec=pltpu.PrefetchScalarGridSpec(
            num_scalar_prefetch=1,
            grid=(),
            in_specs=[VMEM] * (1 + len(ks)) + ([HBM, VMEM] if carried else []),
            out_specs=(HBM, VMEM),
            scratch_shapes=[
                pltpu.VMEM((len(ks), capacity, aux, PAD * PAD), jnp.bfloat16),
                pltpu.VMEM((group, aux, PAD * PAD), jnp.bfloat16),
                pltpu.VMEM((capacity, LANES), jnp.float32),
                pltpu.SemaphoreType.DMA((len(ks) * capacity // group,)),
            ],
        ),
        input_output_aliases={2 + len(ks): 0} if carried else {},
        compiler_params=pltpu.CompilerParams(vmem_limit_bytes=24 * MIB),
        cost_estimate=pl.CostEstimate(flops=0, transcendentals=0, bytes_accessed=len(ks) * 6 * MIB),
    )(meta, table, *[halves[k] for k in ks], *carried)


def per_device(density, vir_coeffs, occ_coeffs, shell_len, mu_shell, nu_shell, owner):
    count = lax.axis_size("rows")
    columns = lax.axis_size("aux")
    position = lax.axis_index("rows").astype(jnp.int32).reshape(1)
    aux, occupied, width = density.shape
    slab = vir_coeffs.shape[0]
    shells = shell_len.shape[1]
    pairs = mu_shell.shape[0]
    capacity = 2 * pairs // count

    packed = whole(
        pack_kernel,
        jax.ShapeDtypeStruct((aux + 2, occupied, width), jnp.bfloat16),
        [density, occ_coeffs, mu_shell.reshape(1, pairs), nu_shell.reshape(1, pairs), owner.reshape(1, pairs)],
        scratch=[pltpu.VMEM((3, 1, pairs), jnp.int32), pltpu.SemaphoreType.DMA((5,))],
        specs=[HBM] * 5,
        limit=60,
    )

    span = occupied * LANES
    source = jnp.arange(span, dtype=jnp.int32)[:, None]
    target = jnp.arange(span, dtype=jnp.int32)[None, :]
    spread = (target == source % LANES * occupied + source // LANES).astype(jnp.bfloat16)
    repeat = (
        jnp.arange(LANES, dtype=jnp.int32)[:, None] == jnp.arange(LANES * PAD, dtype=jnp.int32)[None, :] // PAD
    ).astype(jnp.bfloat16)
    earlier = jnp.arange(shells)[:, None] < jnp.arange(shells)[None, :]
    starts = jnp.sum(jnp.where(earlier[None], shell_len[:, :, None], 0), axis=1)
    starts = (starts + jnp.arange(count, dtype=jnp.int32)[:, None] * slab).reshape(-1)
    digits = jnp.stack([starts // DIGIT, starts % DIGIT, shell_len.reshape(-1)])
    shell_table = jnp.pad(digits, ((0, 5), (0, 0))).astype(jnp.bfloat16)

    half, parts = make_half(position, packed, vir_coeffs, spread, aux)
    state = {}

    def blocks_of(ks, halves):
        state["done"] = make_blocks(
            ks, count, capacity, slab, state["meta"], halves, state["table"], state.get("done")
        )

    def first_blocks(halves):
        state["meta"], state["table"] = make_tables(
            position, parts, shell_table, repeat, pairs, capacity, shells, slab, aux
        )
        blocks_of([0, 1, 2], halves)
        return state["done"][1]

    halves, sums = gather(half, count, "half", first_blocks)
    state["done"] = (state["done"][0], sums)
    blocks_of([3, *range(4, count, 2)], halves)
    for k in range(5, count, 2):
        blocks_of([k], halves)
    blocks, sums = state["done"]
    sums = [sums] + [swap(sums, k, columns, "aux") for k in range(1, columns)]
    while len(sums) > 1:
        sums = [sums[n] + sums[n + 1] for n in range(0, len(sums), 2)]
    pair_scale = jnp.sqrt(sums[0].reshape(-1) / (NAUX * PAD * PAD) + 1e-06)
    return blocks, pair_scale


def solution(mesh):
    return jax.shard_map(
        per_device,
        mesh=mesh,
        in_specs=(
            P("aux", None, "rows"),
            P("rows", None),
            P(None, "rows"),
            P(),
            P("rows"),
            P("rows"),
            P("rows", None),
        ),
        out_specs=(P("rows", "aux", None), P("rows")),
        check_vma=False,
    )
```

```python
import functools

import jax
import jax.numpy as jnp
from jax import lax
from jax.experimental import pallas as pl
from jax.experimental.pallas import tpu as pltpu
from jax.sharding import PartitionSpec as P

NAUX = 128
PAD = 16
LANES = 128
DIGIT = 128
CODE_BITS = 5
CODE = 1 << CODE_BITS
GROUP = 32
MIB = 1 << 20
VMEM = pl.BlockSpec(memory_space=pltpu.VMEM)
HBM = pl.BlockSpec(memory_space=pltpu.HBM)


def swap(x, k, count, axis="rows"):
    return lax.ppermute(x, axis, [(i, i ^ k) for i in range(count)])


def tie(*arrays):
    return lax.optimization_barrier(arrays)


def gather(x, count, name, early):
    parts = {0: x}

    def move(k, value, by):
        with jax.named_scope(f"{name}_{k}"):
            parts[k] = swap(value, by, count)

    for k in (4, 2):
        if k < count:
            move(k, x, k)
    move(1, x, 1)
    x, parts[1] = tie(x, parts[1])
    for k in range(6, count, 2):
        move(k, x, k)
    move(3, parts[2], 1)
    if early is None:
        (parts[4], parts[3]), result = tie(parts[4], parts[3]), None
    else:
        parts[4], parts[3], result = tie(parts[4], parts[3], early(parts))
    for k in range(4, count, 2):
        move(k + 1, parts[k], 1)
    return [parts[k] for k in range(count)], result


def dot(a, b):
    return jnp.dot(a, b, preferred_element_type=jnp.float32)


def dot_t(a, b):
    return lax.dot_general(a, b, (((1,), (1,)), ((), ())), preferred_element_type=jnp.float32)


def whole(body, out_shape, args, scratch=(), scalars=0, specs=None, cost=None, limit=44):
    outs = out_shape if isinstance(out_shape, tuple) else (out_shape,)
    return pl.pallas_call(
        body,
        out_shape=out_shape,
        grid_spec=pltpu.PrefetchScalarGridSpec(
            num_scalar_prefetch=scalars,
            grid=(),
            in_specs=specs or [VMEM] * (len(args) - scalars),
            out_specs=tuple(VMEM for _ in outs) if isinstance(out_shape, tuple) else VMEM,
            scratch_shapes=list(scratch),
        ),
        compiler_params=pltpu.CompilerParams(vmem_limit_bytes=limit * MIB),
        cost_estimate=pl.CostEstimate(flops=0, transcendentals=0, bytes_accessed=cost) if cost else None,
    )(*args)


def pack_kernel(density_ref, occ_ref, mu_ref, nu_ref, owner_ref, out_ref, small_ref, sems):
    aux, occupied, width = density_ref.shape
    pairs = mu_ref.shape[1]
    tiles = width // LANES
    copies = []
    for n, ref in enumerate((mu_ref, nu_ref, owner_ref)):
        copies.append(pltpu.make_async_copy(ref, small_ref.at[n], sems.at[n]))
    for t in range(tiles):
        lanes = pl.ds(t * LANES, LANES)
        copies.append(
            pltpu.make_async_copy(density_ref.at[:, :, lanes], out_ref.at[pl.ds(t * aux, aux)], sems.at[3 + 2 * t])
        )
        copies.append(
            pltpu.make_async_copy(occ_ref.at[:, lanes], out_ref.at[tiles * aux + t], sems.at[4 + 2 * t])
        )
    for copy in copies:
        copy.start()
    for copy in copies[:3]:
        copy.wait()
    mu = small_ref[0]
    digits = [mu // DIGIT, mu % DIGIT, small_ref[1], small_ref[2]]
    per = pairs // LANES
    rows = [d[:, q * LANES : (q + 1) * LANES] for d in digits for q in range(per)]
    rows = jnp.concatenate(rows, axis=0).astype(jnp.float32).astype(jnp.bfloat16)
    for t in range(rows.shape[0] // occupied):
        out_ref[tiles * (aux + 1) + t] = rows[t * occupied : (t + 1) * occupied]
    for copy in copies[3:]:
        copy.wait()


def side_by_side(part_ref, aux, tiles):
    occupied = part_ref.shape[1]
    rows = [part_ref[t * aux : (t + 1) * aux].reshape(aux * occupied, LANES) for t in range(tiles)]
    return jnp.concatenate(rows, axis=1)


def part_kernel(ks, resumed, ahead, aux, where_ref, vir_ref, *refs):
    refs = list(refs)
    blocks = [refs.pop(0) for _ in ks]
    before_ref = refs.pop(0) if resumed else None
    total_ref = refs.pop(0)
    ahead_ref = refs.pop(0) if ahead is not None else None
    columns_ref, sems = refs
    width = columns_ref.shape[2]

    def fetch(k, target, n):
        start = pl.multiple_of((where_ref[0] ^ k) * width, width)
        return pltpu.make_async_copy(vir_ref.at[:, pl.ds(start, width)], target, sems.at[n])

    copies = [fetch(k, columns_ref.at[n], n) for n, k in enumerate(ks)]
    if ahead is not None:
        copies.append(fetch(ahead, ahead_ref, len(ks)))
    for copy in copies:
        copy.start()
    total = None if before_ref is None else before_ref[...]
    for n in range(len(ks)):
        copies[n].wait()
        term = dot_t(side_by_side(blocks[n], aux, width // LANES), columns_ref[n])
        total = term if total is None else total + term
    total_ref[...] = total
    if ahead is not None:
        copies[-1].wait()


def add_part(position, vir, parts, ks, before, ahead, aux):
    slab = vir.shape[0]
    occupied, width = parts[0].shape[1], vir.shape[1] // len(parts)
    out = [jax.ShapeDtypeStruct((aux * occupied, slab), jnp.float32)]
    if ahead is not None:
        out.append(jax.ShapeDtypeStruct((slab, width), vir.dtype))
    args = [position, vir] + [parts[k] for k in ks] + ([] if before is None else [before])
    return whole(
        functools.partial(part_kernel, ks, before is not None, ahead, aux),
        tuple(out),
        args,
        scratch=[
            pltpu.VMEM((len(ks), slab, width), vir.dtype),
            pltpu.SemaphoreType.DMA((len(ks) + 1,)),
        ],
        scalars=1,
        specs=[HBM] + [VMEM] * (len(args) - 2),
        cost=len(ks) * 2 * MIB,
    )


def half_kernel(aux, before_ref, part_ref, column_ref, spread_ref, out_ref, total_ref):
    occupied, width = part_ref.shape[1], column_ref.shape[1]
    tiles = total_ref.shape[0]
    total = before_ref[...] + dot_t(side_by_side(part_ref, aux, width // LANES), column_ref[...])
    for t in range(tiles):
        total_ref[t] = total[:, t * LANES : (t + 1) * LANES]
    columns = []
    for i in range(occupied):
        h = [total_ref[t, pl.ds(i, aux, stride=occupied), :].astype(jnp.bfloat16) for t in range(tiles)]
        columns.append(jnp.concatenate(h, axis=0))
    mixed = dot(jnp.concatenate(columns, axis=1), spread_ref[...]).astype(jnp.bfloat16)
    wide = occupied * LANES
    for t in range(tiles):
        out_ref[:, t * wide : (t + 1) * wide] = mixed[t * aux : (t + 1) * aux]


def make_half(position, packed, vir, spread, aux):
    count = lax.axis_size("rows")
    slab = vir.shape[0]
    occupied = packed.shape[1]
    order = [0, 1, 2, 3] + list(range(4, count, 2)) + list(range(5, count, 2))
    early, middle, last = order[:4], order[4:-1], order[-1]
    parts, _ = gather(packed, count, "density", None)
    [total] = add_part(position, vir, parts, early, None, None, aux)
    total, column = add_part(position, vir, parts, middle, total, last, aux)
    half = whole(
        functools.partial(half_kernel, aux),
        jax.ShapeDtypeStruct((aux, slab * occupied), jnp.bfloat16),
        [total, parts[last], column, spread],
        scratch=[pltpu.VMEM((slab // LANES, aux * occupied, LANES), jnp.float32)],
        cost=4 * MIB,
    )
    return half, parts


def table_kernel(count, pairs, capacity, shells, slab, width, where_ref, *refs):
    parts, (shell_ref, repeat_ref, meta_ref, table_ref, digit_ref, small_ref, sems) = refs[:count], refs[count:]
    occupied = parts[0].shape[1]
    tiles = width // LANES
    extra = small_ref.shape[1]
    first_extra = parts[0].shape[0] - extra
    copies = [
        pltpu.make_async_copy(parts[k].at[pl.ds(first_extra, extra)], small_ref.at[k], sems.at[k]) for k in range(count)
    ]
    for copy in copies:
        copy.start()
    for k in range(count):
        copies[k].wait()
        first = (where_ref[0] ^ k) * (tiles * PAD)
        occ = jnp.concatenate([small_ref[k, t] for t in range(tiles)], axis=0)
        spread = dot(occ, repeat_ref[...])
        for t in range(tiles):
            for q in range(PAD):
                table_ref[first + t * PAD + q] = spread[
                    t * occupied : (t + 1) * occupied, q * LANES : (q + 1) * LANES
                ]
        for t in range(extra - tiles):
            digit_ref[k, t * occupied : (t + 1) * occupied] = small_ref[k, tiles + t].astype(jnp.float32)
    last = count * tiles * PAD
    table_ref[last] = jnp.zeros((occupied, LANES), jnp.float32)
    table_ref[last + 1] = jnp.zeros((occupied, LANES), jnp.float32)
    meta_ref[2 * count :, :] = jnp.full((meta_ref.shape[0] - 2 * count, LANES), where_ref[0], jnp.int32)

    per = pairs // LANES
    total = shell_ref.shape[1]
    f32, bf16 = jnp.float32, jnp.bfloat16
    before = (
        lax.broadcasted_iota(jnp.int32, (pairs, pairs), 0) < lax.broadcasted_iota(jnp.int32, (pairs, pairs), 1)
    ).astype(f32).astype(bf16)
    number = lax.broadcasted_iota(jnp.int32, (total, pairs), 0).astype(f32)
    slot = lax.broadcasted_iota(jnp.int32, (LANES, pairs), 0).astype(f32)
    place = where_ref[0].astype(f32)

    def body(k, carry):
        source = (where_ref[0] ^ k).astype(f32)
        rows = digit_ref[k]
        d = [jnp.concatenate([rows[n * per + q : n * per + q + 1] for q in range(per)], axis=1) for n in range(4)]
        mu = d[0] * DIGIT + d[1]
        nu = d[2] + source * shells
        mine = jnp.where(d[3] == place, 1.0, 0.0)
        rank = dot(jnp.broadcast_to(mine, (8, pairs)).astype(bf16), before)[:1]
        rank = jnp.where(mine > 0, rank, -1.0)
        found = []
        for wanted in (mu, nu):
            hits = jnp.where(number == wanted, 1.0, 0.0).astype(bf16)
            found.append(dot(shell_ref[...], hits).astype(bf16))
        placed = [
            jnp.where((slot == rank + shift) & (rank >= 0), 1.0, 0.0).astype(bf16) for shift in (0, capacity)
        ]
        mixed = dot_t(found[0], placed[0]) + dot_t(found[1], placed[1])
        start = mixed[0:1] * DIGIT + mixed[1:2]
        number_of = lax.broadcasted_iota(jnp.int32, (1, LANES), 1)
        start = jnp.where(number_of < capacity, start, jnp.maximum(start - source * slab, 0.0))
        code = (start * CODE + mixed[2:3]).astype(jnp.int32)
        meta_ref[pl.ds(k, 1), :] = code
        live = jnp.sum(mine, axis=1, keepdims=True).astype(jnp.int32)
        meta_ref[pl.ds(count + k, 1), :] = jnp.broadcast_to(live, (1, LANES))
        return carry

    lax.fori_loop(0, count, body, 0)


def make_tables(position, parts, shell_table, repeat, pairs, capacity, shells, slab, width):
    count = len(parts)
    occupied = parts[0].shape[1]
    tiles = width // LANES
    digits = 4 * pairs // LANES
    extra = tiles + digits // occupied
    return whole(
        functools.partial(table_kernel, count, pairs, capacity, shells, slab, width),
        (
            jax.ShapeDtypeStruct((2 * count + 8, LANES), jnp.int32),
            jax.ShapeDtypeStruct((count * width // 8 + 2, occupied, LANES), jnp.float32),
        ),
        [position, *parts, shell_table, repeat],
        scratch=[
            pltpu.VMEM((count, digits, LANES), jnp.float32),
            pltpu.VMEM((count, extra, occupied, LANES), jnp.bfloat16),
            pltpu.SemaphoreType.DMA((count,)),
        ],
        scalars=1,
        specs=[HBM] * count + [VMEM] * 2,
        cost=16 * MIB,
    )


def window(ref, tile, shift, lane):
    top = ref.shape[1] // LANES - 1
    tiles = [ref[:, pl.ds(pl.multiple_of(t * LANES, LANES), LANES)] for t in (tile, jnp.minimum(tile + 1, top))]
    turned = [pltpu.roll(t.astype(jnp.float32), (LANES - shift) & (LANES - 1), 1) for t in tiles]
    return jnp.where(lane < LANES - shift, turned[0], turned[1]).astype(jnp.bfloat16)


def ship(ks, held_ref, out_ref, sems, place, capacity):
    copies = []
    for n, k in enumerate(ks):
        target = out_ref.at[pl.ds((place ^ k) * capacity, capacity)]
        copies.append(pltpu.make_async_copy(held_ref.at[n], target, sems.at[n]))
    return copies


def ship_kernel(ks, count, capacity, meta_ref, held_ref, _, out_ref, sems):
    copies = ship(ks, held_ref, out_ref, sems, meta_ref[2 * count, 0], capacity)
    for copy in copies:
        copy.start()
    for copy in copies:
        copy.wait()


def block_kernel(ks, old_ks, resumed, group, count, capacity, meta_ref, table_ref, *refs):
    refs = list(refs)
    halves = [refs.pop(0) for _ in ks]
    old_sum_ref, old_held_ref = (refs.pop(0), refs.pop(0)) if old_ks else (None, None)
    if resumed:
        refs.pop(0)
    held_ref, sum_ref = refs.pop(0), refs.pop(0)
    out_ref = refs.pop(0) if old_ks else None
    square_ref, sems = refs
    aux = halves[0].shape[0]
    occupied = table_ref.shape[1]
    per = LANES // occupied
    per_bits = per.bit_length() - 1
    lane = lax.broadcasted_iota(jnp.int32, (occupied, LANES), 1)
    column = lane % PAD
    wide_lane = lax.broadcasted_iota(jnp.int32, (aux, LANES), 1)
    ones = jnp.ones((8, LANES), jnp.float32)
    place = meta_ref[2 * count, 0]
    copies = ship(old_ks, old_held_ref, out_ref, sems, place, capacity) if old_ks else []
    for copy in copies:
        copy.start()
    sum_ref[...] = old_sum_ref[...] if old_ks else jnp.zeros(sum_ref.shape, jnp.float32)

    for n, k in enumerate(ks):
        live = meta_ref[count + k, 0]

        @pl.loop(0, capacity // group)
        def _(turn, n=n, k=k, live=live):
            at = turn * group

            @pl.when(at < live)
            def _():
                for s in range(group):
                    mu, nu = meta_ref[k, at + s], meta_ref[k, capacity + at + s]
                    mu_wide, nu_length = (mu & (CODE - 1)) * PAD, nu & (CODE - 1)
                    nu_tile, nu_shift = nu >> (CODE_BITS + per_bits), (nu >> CODE_BITS) & (per - 1)
                    left = window(halves[n], nu_tile, nu_shift * occupied, wide_lane)
                    tile, shift = mu >> (CODE_BITS + 3), ((mu >> CODE_BITS) & 7) * PAD
                    back = (LANES - shift) & (LANES - 1)
                    x = [pltpu.roll(table_ref[tile + q], back, 1) for q in range(3)]
                    keep = lane < LANES - shift
                    coeff = []
                    for q in range(2):
                        valid = (column < nu_length) & (lane + q * LANES < mu_wide)
                        coeff.append(jnp.where(valid, jnp.where(keep, x[q], x[q + 1]), 0.0))
                    right = [
                        jnp.concatenate([jnp.where(column == m, c, 0.0) for m in range(PAD)], axis=0) for c in coeff
                    ]
                    right = jnp.concatenate(right, axis=1).astype(jnp.bfloat16)
                    block = dot(left, right).astype(jnp.bfloat16)
                    held_ref[n, at + s] = block
                    flat = block.astype(jnp.float32)
                    total = jnp.sum(flat * flat, axis=0, keepdims=True)
                    square_ref[pl.ds(at + s, 1), :] = total[:, :LANES] + total[:, LANES:]

            @pl.when(at >= live)
            def _():
                square_ref[pl.ds(at, group), :] = jnp.zeros((group, LANES), jnp.float32)
                held_ref[n, pl.ds(at, group)] = jnp.zeros((group, aux, PAD * PAD), jnp.bfloat16)

        sums = lax.dot_general(
            ones,
            square_ref[...],
            (((1,), (1,)), ((), ())),
            precision=lax.Precision.HIGHEST,
            preferred_element_type=jnp.float32,
        )
        sum_ref[pl.ds(place ^ k, 1), :] = sums[:1]

    for copy in copies:
        copy.wait()


def make_blocks(ks, count, capacity, meta, halves, table, done):
    aux = halves[ks[0]].shape[0]
    old_ks, sums, held, out = done or ([], None, None, None)
    carried = [] if not old_ks else [sums, held] + ([] if out is None else [out])
    shapes = [
        jax.ShapeDtypeStruct((len(ks), capacity, aux, PAD * PAD), jnp.bfloat16),
        jax.ShapeDtypeStruct((count, capacity), jnp.float32),
    ]
    if old_ks:
        shapes.append(jax.ShapeDtypeStruct((count * capacity, aux, PAD * PAD), jnp.bfloat16))
    result = pl.pallas_call(
        functools.partial(block_kernel, ks, old_ks, out is not None, min(GROUP, capacity), count, capacity),
        out_shape=tuple(shapes),
        grid_spec=pltpu.PrefetchScalarGridSpec(
            num_scalar_prefetch=1,
            grid=(),
            in_specs=[VMEM] * (1 + len(ks) + min(len(carried), 2)) + [HBM] * (out is not None),
            out_specs=(VMEM, VMEM, HBM)[: len(shapes)],
            scratch_shapes=[
                pltpu.VMEM((capacity, LANES), jnp.float32),
                pltpu.SemaphoreType.DMA((max(len(old_ks), 1),)),
            ],
        ),
        input_output_aliases={} if out is None else {4 + len(ks): 2},
        compiler_params=pltpu.CompilerParams(vmem_limit_bytes=24 * MIB),
        cost_estimate=pl.CostEstimate(flops=0, transcendentals=0, bytes_accessed=len(ks) * 6 * MIB),
    )(meta, table, *[halves[k] for k in ks], *carried)
    return ks, result[1], result[0], result[2] if old_ks else None


def make_output(count, capacity, meta, done):
    ks, _, held, out = done
    return pl.pallas_call(
        functools.partial(ship_kernel, ks, count, capacity),
        out_shape=jax.ShapeDtypeStruct(out.shape, out.dtype),
        grid_spec=pltpu.PrefetchScalarGridSpec(
            num_scalar_prefetch=1,
            grid=(),
            in_specs=[VMEM, HBM],
            out_specs=HBM,
            scratch_shapes=[pltpu.SemaphoreType.DMA((len(ks),))],
        ),
        input_output_aliases={2: 0},
        compiler_params=pltpu.CompilerParams(vmem_limit_bytes=24 * MIB),
        cost_estimate=pl.CostEstimate(flops=0, transcendentals=0, bytes_accessed=4 * MIB),
    )(meta, held, out)


def per_device(density, vir_coeffs, occ_coeffs, shell_len, mu_shell, nu_shell, owner):
    count = lax.axis_size("rows")
    columns = lax.axis_size("aux")
    position = lax.axis_index("rows").astype(jnp.int32).reshape(1)
    aux, occupied, width = density.shape
    slab = vir_coeffs.shape[0]
    shells = shell_len.shape[1]
    pairs = mu_shell.shape[0]
    capacity = 2 * pairs // count

    tiles = width // LANES
    rows = tiles * (aux + 1) + 4 * pairs // (LANES * occupied)
    packed = whole(
        pack_kernel,
        jax.ShapeDtypeStruct((rows, occupied, LANES), jnp.bfloat16),
        [density, occ_coeffs, mu_shell.reshape(1, pairs), nu_shell.reshape(1, pairs), owner.reshape(1, pairs)],
        scratch=[pltpu.VMEM((3, 1, pairs), jnp.int32), pltpu.SemaphoreType.DMA((3 + 2 * tiles,))],
        specs=[HBM] * 5,
        limit=60,
    )

    span = occupied * LANES
    source = jnp.arange(span, dtype=jnp.int32)[:, None]
    target = jnp.arange(span, dtype=jnp.int32)[None, :]
    spread = (target == source % LANES * occupied + source // LANES).astype(jnp.bfloat16)
    repeat = (
        jnp.arange(LANES, dtype=jnp.int32)[:, None] == jnp.arange(LANES * PAD, dtype=jnp.int32)[None, :] // PAD
    ).astype(jnp.bfloat16)
    earlier = jnp.arange(shells)[:, None] < jnp.arange(shells)[None, :]
    starts = jnp.sum(jnp.where(earlier[None], shell_len[:, :, None], 0), axis=1)
    starts = (starts + jnp.arange(count, dtype=jnp.int32)[:, None] * slab).reshape(-1)
    digits = jnp.stack([starts // DIGIT, starts % DIGIT, shell_len.reshape(-1)])
    shell_table = jnp.pad(digits, ((0, 5), (0, 0))).astype(jnp.bfloat16)

    half, parts = make_half(position, packed, vir_coeffs, spread, aux)
    state = {}

    def blocks_of(ks, halves):
        state["done"] = make_blocks(ks, count, capacity, state["meta"], halves, state["table"], state.get("done"))

    def first_blocks(halves):
        state["meta"], state["table"] = make_tables(
            position, parts, shell_table, repeat, pairs, capacity, shells, slab, width
        )
        blocks_of([0, 1, 2], halves)
        return state["done"][1]

    halves, sums = gather(half, count, "half", first_blocks)
    ks, _, held, out = state["done"]
    state["done"] = (ks, sums, held, out)
    blocks_of([3, *range(4, count, 2)], halves)
    for k in range(5, count, 2):
        blocks_of([k], halves)
    sums = state["done"][1]
    blocks = make_output(count, capacity, state["meta"], state["done"])
    sums = [sums] + [swap(sums, k, columns, "aux") for k in range(1, columns)]
    while len(sums) > 1:
        sums = [sums[n] + sums[n + 1] for n in range(0, len(sums), 2)]
    pair_scale = jnp.sqrt(sums[0].reshape(-1) / (NAUX * PAD * PAD) + 1e-06)
    return blocks, pair_scale


def solution(mesh):
    return jax.shard_map(
        per_device,
        mesh=mesh,
        in_specs=(
            P("aux", None, "rows"),
            P("rows", None),
            P(None, "rows"),
            P(),
            P("rows"),
            P("rows"),
            P("rows", None),
        ),
        out_specs=(P("rows", "aux", None), P("rows")),
        check_vma=False,
    )
```

```python
import functools

import jax
import jax.numpy as jnp
from jax import lax
from jax.experimental import pallas as pl
from jax.experimental.pallas import tpu as pltpu
from jax.sharding import PartitionSpec as P

NAUX = 128
PAD = 16
LANES = 128
DIGIT = 128
CODE_BITS = 5
CODE = 1 << CODE_BITS
GROUP = 64
MIB = 1 << 20
VMEM = pl.BlockSpec(memory_space=pltpu.VMEM)
HBM = pl.BlockSpec(memory_space=pltpu.HBM)


def swap(x, k, count, axis="rows"):
    return lax.ppermute(x, axis, [(i, i ^ k) for i in range(count)])


def tie(*arrays):
    return lax.optimization_barrier(arrays)


def gather(x, count, name, early):
    parts = {0: x}

    def move(k, value, by):
        with jax.named_scope(f"{name}_{k}"):
            parts[k] = swap(value, by, count)

    for k in (4, 2):
        if k < count:
            move(k, x, k)
    move(1, x, 1)
    x, parts[1] = tie(x, parts[1])
    for k in range(6, count, 2):
        move(k, x, k)
    move(3, parts[2], 1)
    if early is None:
        (parts[4], parts[3]), result = tie(parts[4], parts[3]), None
    else:
        parts[4], parts[3], result = tie(parts[4], parts[3], early(parts))
    for k in range(4, count, 2):
        move(k + 1, parts[k], 1)
    return [parts[k] for k in range(count)], result


def dot(a, b):
    return jnp.dot(a, b, preferred_element_type=jnp.float32)


def dot_t(a, b):
    return lax.dot_general(a, b, (((1,), (1,)), ((), ())), preferred_element_type=jnp.float32)


def whole(body, out_shape, args, scratch=(), scalars=0, specs=None, cost=None, limit=44):
    outs = out_shape if isinstance(out_shape, tuple) else (out_shape,)
    return pl.pallas_call(
        body,
        out_shape=out_shape,
        grid_spec=pltpu.PrefetchScalarGridSpec(
            num_scalar_prefetch=scalars,
            grid=(),
            in_specs=specs or [VMEM] * (len(args) - scalars),
            out_specs=tuple(VMEM for _ in outs) if isinstance(out_shape, tuple) else VMEM,
            scratch_shapes=list(scratch),
        ),
        compiler_params=pltpu.CompilerParams(vmem_limit_bytes=limit * MIB),
        cost_estimate=pl.CostEstimate(flops=0, transcendentals=0, bytes_accessed=cost) if cost else None,
    )(*args)


def pack_kernel(density_ref, occ_ref, mu_ref, nu_ref, owner_ref, out_ref, small_ref, sems):
    aux, occupied, width = density_ref.shape
    pairs = mu_ref.shape[1]
    tiles = width // LANES
    copies = []
    for n, ref in enumerate((mu_ref, nu_ref, owner_ref)):
        copies.append(pltpu.make_async_copy(ref, small_ref.at[n], sems.at[n]))
    for t in range(tiles):
        lanes = pl.ds(t * LANES, LANES)
        copies.append(
            pltpu.make_async_copy(density_ref.at[:, :, lanes], out_ref.at[pl.ds(t * aux, aux)], sems.at[3 + 2 * t])
        )
        copies.append(
            pltpu.make_async_copy(occ_ref.at[:, lanes], out_ref.at[tiles * aux + t], sems.at[4 + 2 * t])
        )
    for copy in copies:
        copy.start()
    for copy in copies[:3]:
        copy.wait()
    mu = small_ref[0]
    digits = [mu // DIGIT, mu % DIGIT, small_ref[1], small_ref[2]]
    per = pairs // LANES
    rows = [d[:, q * LANES : (q + 1) * LANES] for d in digits for q in range(per)]
    rows = jnp.concatenate(rows, axis=0).astype(jnp.float32).astype(jnp.bfloat16)
    for t in range(rows.shape[0] // occupied):
        out_ref[tiles * (aux + 1) + t] = rows[t * occupied : (t + 1) * occupied]
    for copy in copies[3:]:
        copy.wait()


def side_by_side(part_ref, aux, tiles):
    occupied = part_ref.shape[1]
    rows = [part_ref[t * aux : (t + 1) * aux].reshape(aux * occupied, LANES) for t in range(tiles)]
    return jnp.concatenate(rows, axis=1)


def part_kernel(ks, resumed, ahead, aux, where_ref, vir_ref, *refs):
    refs = list(refs)
    blocks = [refs.pop(0) for _ in ks]
    before_ref = refs.pop(0) if resumed else None
    total_ref = refs.pop(0)
    ahead_ref = refs.pop(0) if ahead is not None else None
    columns_ref, sems = refs
    width = columns_ref.shape[2]

    def fetch(k, target, n):
        start = pl.multiple_of((where_ref[0] ^ k) * width, width)
        return pltpu.make_async_copy(vir_ref.at[:, pl.ds(start, width)], target, sems.at[n])

    copies = [fetch(k, columns_ref.at[n], n) for n, k in enumerate(ks)]
    if ahead is not None:
        copies.append(fetch(ahead, ahead_ref, len(ks)))
    for copy in copies:
        copy.start()
    total = None if before_ref is None else before_ref[...]
    for n in range(len(ks)):
        copies[n].wait()
        term = dot_t(side_by_side(blocks[n], aux, width // LANES), columns_ref[n])
        total = term if total is None else total + term
    total_ref[...] = total
    if ahead is not None:
        copies[-1].wait()


def add_part(position, vir, parts, ks, before, ahead, aux):
    slab = vir.shape[0]
    occupied, width = parts[0].shape[1], vir.shape[1] // len(parts)
    out = [jax.ShapeDtypeStruct((aux * occupied, slab), jnp.float32)]
    if ahead is not None:
        out.append(jax.ShapeDtypeStruct((slab, width), vir.dtype))
    args = [position, vir] + [parts[k] for k in ks] + ([] if before is None else [before])
    return whole(
        functools.partial(part_kernel, ks, before is not None, ahead, aux),
        tuple(out),
        args,
        scratch=[
            pltpu.VMEM((len(ks), slab, width), vir.dtype),
            pltpu.SemaphoreType.DMA((len(ks) + 1,)),
        ],
        scalars=1,
        specs=[HBM] + [VMEM] * (len(args) - 2),
        cost=len(ks) * 2 * MIB,
    )


def half_kernel(aux, before_ref, part_ref, column_ref, spread_ref, out_ref, total_ref):
    occupied, width = part_ref.shape[1], column_ref.shape[1]
    tiles = total_ref.shape[0]
    total = before_ref[...] + dot_t(side_by_side(part_ref, aux, width // LANES), column_ref[...])
    for t in range(tiles):
        total_ref[t] = total[:, t * LANES : (t + 1) * LANES]
    columns = []
    for i in range(occupied):
        h = [total_ref[t, pl.ds(i, aux, stride=occupied), :].astype(jnp.bfloat16) for t in range(tiles)]
        columns.append(jnp.concatenate(h, axis=0))
    mixed = dot(jnp.concatenate(columns, axis=1), spread_ref[...]).astype(jnp.bfloat16)
    wide = occupied * LANES
    for t in range(tiles):
        out_ref[:, t * wide : (t + 1) * wide] = mixed[t * aux : (t + 1) * aux]


def make_half(position, packed, vir, spread, aux):
    count = lax.axis_size("rows")
    slab = vir.shape[0]
    occupied = packed.shape[1]
    order = [0, 1, 2, 3] + list(range(4, count, 2)) + list(range(5, count, 2))
    early, middle, last = order[:4], order[4:-1], order[-1]
    parts, _ = gather(packed, count, "density", None)
    [total] = add_part(position, vir, parts, early, None, None, aux)
    total, column = add_part(position, vir, parts, middle, total, last, aux)
    half = whole(
        functools.partial(half_kernel, aux),
        jax.ShapeDtypeStruct((aux, slab * occupied), jnp.bfloat16),
        [total, parts[last], column, spread],
        scratch=[pltpu.VMEM((slab // LANES, aux * occupied, LANES), jnp.float32)],
        cost=4 * MIB,
    )
    return half, parts


def table_kernel(count, pairs, capacity, shells, slab, width, where_ref, *refs):
    parts, (shell_ref, repeat_ref, meta_ref, table_ref, digit_ref, small_ref, sems) = refs[:count], refs[count:]
    occupied = parts[0].shape[1]
    tiles = width // LANES
    extra = small_ref.shape[1]
    first_extra = parts[0].shape[0] - extra
    copies = [
        pltpu.make_async_copy(parts[k].at[pl.ds(first_extra, extra)], small_ref.at[k], sems.at[k]) for k in range(count)
    ]
    for copy in copies:
        copy.start()
    for k in range(count):
        copies[k].wait()
        first = (where_ref[0] ^ k) * (tiles * PAD)
        occ = jnp.concatenate([small_ref[k, t] for t in range(tiles)], axis=0)
        spread = dot(occ, repeat_ref[...])
        for t in range(tiles):
            for q in range(PAD):
                table_ref[first + t * PAD + q] = spread[
                    t * occupied : (t + 1) * occupied, q * LANES : (q + 1) * LANES
                ]
        for t in range(extra - tiles):
            digit_ref[k, t * occupied : (t + 1) * occupied] = small_ref[k, tiles + t].astype(jnp.float32)
    last = count * tiles * PAD
    table_ref[last] = jnp.zeros((occupied, LANES), jnp.float32)
    table_ref[last + 1] = jnp.zeros((occupied, LANES), jnp.float32)
    meta_ref[2 * count :, :] = jnp.full((meta_ref.shape[0] - 2 * count, LANES), where_ref[0], jnp.int32)

    per = pairs // LANES
    total = shell_ref.shape[1]
    f32, bf16 = jnp.float32, jnp.bfloat16
    before = (
        lax.broadcasted_iota(jnp.int32, (pairs, pairs), 0) < lax.broadcasted_iota(jnp.int32, (pairs, pairs), 1)
    ).astype(f32).astype(bf16)
    number = lax.broadcasted_iota(jnp.int32, (total, pairs), 0).astype(f32)
    slot = lax.broadcasted_iota(jnp.int32, (LANES, pairs), 0).astype(f32)
    place = where_ref[0].astype(f32)

    def body(k, carry):
        source = (where_ref[0] ^ k).astype(f32)
        rows = digit_ref[k]
        d = [jnp.concatenate([rows[n * per + q : n * per + q + 1] for q in range(per)], axis=1) for n in range(4)]
        mu = d[0] * DIGIT + d[1]
        nu = d[2] + source * shells
        mine = jnp.where(d[3] == place, 1.0, 0.0)
        rank = dot(jnp.broadcast_to(mine, (8, pairs)).astype(bf16), before)[:1]
        rank = jnp.where(mine > 0, rank, -1.0)
        found = []
        for wanted in (mu, nu):
            hits = jnp.where(number == wanted, 1.0, 0.0).astype(bf16)
            found.append(dot(shell_ref[...], hits).astype(bf16))
        placed = [
            jnp.where((slot == rank + shift) & (rank >= 0), 1.0, 0.0).astype(bf16) for shift in (0, capacity)
        ]
        mixed = dot_t(found[0], placed[0]) + dot_t(found[1], placed[1])
        start = mixed[0:1] * DIGIT + mixed[1:2]
        number_of = lax.broadcasted_iota(jnp.int32, (1, LANES), 1)
        start = jnp.where(number_of < capacity, start, jnp.maximum(start - source * slab, 0.0))
        code = (start * CODE + mixed[2:3]).astype(jnp.int32)
        meta_ref[pl.ds(k, 1), :] = code
        live = jnp.sum(mine, axis=1, keepdims=True).astype(jnp.int32)
        meta_ref[pl.ds(count + k, 1), :] = jnp.broadcast_to(live, (1, LANES))
        return carry

    lax.fori_loop(0, count, body, 0)


def make_tables(position, parts, shell_table, repeat, pairs, capacity, shells, slab, width):
    count = len(parts)
    occupied = parts[0].shape[1]
    tiles = width // LANES
    digits = 4 * pairs // LANES
    extra = tiles + digits // occupied
    return whole(
        functools.partial(table_kernel, count, pairs, capacity, shells, slab, width),
        (
            jax.ShapeDtypeStruct((2 * count + 8, LANES), jnp.int32),
            jax.ShapeDtypeStruct((count * width // 8 + 2, occupied, LANES), jnp.float32),
        ),
        [position, *parts, shell_table, repeat],
        scratch=[
            pltpu.VMEM((count, digits, LANES), jnp.float32),
            pltpu.VMEM((count, extra, occupied, LANES), jnp.bfloat16),
            pltpu.SemaphoreType.DMA((count,)),
        ],
        scalars=1,
        specs=[HBM] * count + [VMEM] * 2,
        cost=16 * MIB,
    )


def window(ref, tile, shift, lane):
    top = ref.shape[1] // LANES - 1
    tiles = [ref[:, pl.ds(pl.multiple_of(t * LANES, LANES), LANES)] for t in (tile, jnp.minimum(tile + 1, top))]
    turned = [pltpu.roll(t.astype(jnp.float32), (LANES - shift) & (LANES - 1), 1) for t in tiles]
    return jnp.where(lane < LANES - shift, turned[0], turned[1]).astype(jnp.bfloat16)


def ship(ks, held_ref, out_ref, sems, place, capacity):
    copies = []
    for n, k in enumerate(ks):
        target = out_ref.at[pl.ds((place ^ k) * capacity, capacity)]
        copies.append(pltpu.make_async_copy(held_ref.at[n], target, sems.at[n]))
    return copies


def ship_kernel(ks, count, capacity, meta_ref, held_ref, _, out_ref, sems):
    copies = ship(ks, held_ref, out_ref, sems, meta_ref[2 * count, 0], capacity)
    for copy in copies:
        copy.start()
    for copy in copies:
        copy.wait()


def block_kernel(ks, old_ks, resumed, group, count, capacity, meta_ref, table_ref, *refs):
    refs = list(refs)
    halves = [refs.pop(0) for _ in ks]
    old_sum_ref, old_held_ref = (refs.pop(0), refs.pop(0)) if old_ks else (None, None)
    if resumed:
        refs.pop(0)
    held_ref, sum_ref = refs.pop(0), refs.pop(0)
    out_ref = refs.pop(0) if old_ks else None
    square_ref, sems = refs
    aux = halves[0].shape[0]
    occupied = table_ref.shape[1]
    per = LANES // occupied
    per_bits = per.bit_length() - 1
    lane = lax.broadcasted_iota(jnp.int32, (occupied, LANES), 1)
    column = lane % PAD
    wide_lane = lax.broadcasted_iota(jnp.int32, (aux, LANES), 1)
    ones = jnp.ones((8, LANES), jnp.float32)
    place = meta_ref[2 * count, 0]
    copies = ship(old_ks, old_held_ref, out_ref, sems, place, capacity) if old_ks else []
    for copy in copies:
        copy.start()
    sum_ref[...] = old_sum_ref[...] if old_ks else jnp.zeros(sum_ref.shape, jnp.float32)

    for n, k in enumerate(ks):
        live = meta_ref[count + k, 0]

        @pl.loop(0, capacity // group)
        def _(turn, n=n, k=k, live=live):
            at = turn * group

            @pl.when(at < live)
            def _():
                for s in range(group):
                    mu, nu = meta_ref[k, at + s], meta_ref[k, capacity + at + s]
                    mu_wide, nu_length = (mu & (CODE - 1)) * PAD, nu & (CODE - 1)
                    nu_tile, nu_shift = nu >> (CODE_BITS + per_bits), (nu >> CODE_BITS) & (per - 1)
                    left = window(halves[n], nu_tile, nu_shift * occupied, wide_lane)
                    tile, shift = mu >> (CODE_BITS + 3), ((mu >> CODE_BITS) & 7) * PAD
                    back = (LANES - shift) & (LANES - 1)
                    x = [pltpu.roll(table_ref[tile + q], back, 1) for q in range(3)]
                    keep = lane < LANES - shift
                    coeff = []
                    for q in range(2):
                        valid = (column < nu_length) & (lane + q * LANES < mu_wide)
                        coeff.append(jnp.where(valid, jnp.where(keep, x[q], x[q + 1]), 0.0))
                    right = [
                        jnp.concatenate([jnp.where(column == m, c, 0.0) for m in range(PAD)], axis=0) for c in coeff
                    ]
                    right = jnp.concatenate(right, axis=1).astype(jnp.bfloat16)
                    block = dot(left, right).astype(jnp.bfloat16)
                    held_ref[n, at + s] = block
                    flat = block.astype(jnp.float32)
                    total = jnp.sum(flat * flat, axis=0, keepdims=True)
                    square_ref[pl.ds(at + s, 1), :] = total[:, :LANES] + total[:, LANES:]

            @pl.when(at >= live)
            def _():
                square_ref[pl.ds(at, group), :] = jnp.zeros((group, LANES), jnp.float32)
                held_ref[n, pl.ds(at, group)] = jnp.zeros((group, aux, PAD * PAD), jnp.bfloat16)

        sums = lax.dot_general(
            ones,
            square_ref[...],
            (((1,), (1,)), ((), ())),
            precision=lax.Precision.HIGHEST,
            preferred_element_type=jnp.float32,
        )
        sum_ref[pl.ds(place ^ k, 1), :] = sums[:1]

    for copy in copies:
        copy.wait()


def make_blocks(ks, count, capacity, meta, halves, table, done):
    aux = halves[ks[0]].shape[0]
    old_ks, sums, held, out = done or ([], None, None, None)
    carried = [] if not old_ks else [sums, held] + ([] if out is None else [out])
    shapes = [
        jax.ShapeDtypeStruct((len(ks), capacity, aux, PAD * PAD), jnp.bfloat16),
        jax.ShapeDtypeStruct((count, capacity), jnp.float32),
    ]
    if old_ks:
        shapes.append(jax.ShapeDtypeStruct((count * capacity, aux, PAD * PAD), jnp.bfloat16))
    result = pl.pallas_call(
        functools.partial(block_kernel, ks, old_ks, out is not None, min(GROUP, capacity), count, capacity),
        out_shape=tuple(shapes),
        grid_spec=pltpu.PrefetchScalarGridSpec(
            num_scalar_prefetch=1,
            grid=(),
            in_specs=[VMEM] * (1 + len(ks) + min(len(carried), 2)) + [HBM] * (out is not None),
            out_specs=(VMEM, VMEM, HBM)[: len(shapes)],
            scratch_shapes=[
                pltpu.VMEM((capacity, LANES), jnp.float32),
                pltpu.SemaphoreType.DMA((max(len(old_ks), 1),)),
            ],
        ),
        input_output_aliases={} if out is None else {4 + len(ks): 2},
        compiler_params=pltpu.CompilerParams(vmem_limit_bytes=24 * MIB),
        cost_estimate=pl.CostEstimate(flops=0, transcendentals=0, bytes_accessed=len(ks) * 6 * MIB),
    )(meta, table, *[halves[k] for k in ks], *carried)
    return ks, result[1], result[0], result[2] if old_ks else None


def make_output(count, capacity, meta, done):
    ks, _, held, out = done
    return pl.pallas_call(
        functools.partial(ship_kernel, ks, count, capacity),
        out_shape=jax.ShapeDtypeStruct(out.shape, out.dtype),
        grid_spec=pltpu.PrefetchScalarGridSpec(
            num_scalar_prefetch=1,
            grid=(),
            in_specs=[VMEM, HBM],
            out_specs=HBM,
            scratch_shapes=[pltpu.SemaphoreType.DMA((len(ks),))],
        ),
        input_output_aliases={2: 0},
        compiler_params=pltpu.CompilerParams(vmem_limit_bytes=24 * MIB),
        cost_estimate=pl.CostEstimate(flops=0, transcendentals=0, bytes_accessed=4 * MIB),
    )(meta, held, out)


def per_device(density, vir_coeffs, occ_coeffs, shell_len, mu_shell, nu_shell, owner):
    count = lax.axis_size("rows")
    columns = lax.axis_size("aux")
    position = lax.axis_index("rows").astype(jnp.int32).reshape(1)
    aux, occupied, width = density.shape
    slab = vir_coeffs.shape[0]
    shells = shell_len.shape[1]
    pairs = mu_shell.shape[0]
    capacity = 2 * pairs // count

    tiles = width // LANES
    rows = tiles * (aux + 1) + 4 * pairs // (LANES * occupied)
    packed = whole(
        pack_kernel,
        jax.ShapeDtypeStruct((rows, occupied, LANES), jnp.bfloat16),
        [density, occ_coeffs, mu_shell.reshape(1, pairs), nu_shell.reshape(1, pairs), owner.reshape(1, pairs)],
        scratch=[pltpu.VMEM((3, 1, pairs), jnp.int32), pltpu.SemaphoreType.DMA((3 + 2 * tiles,))],
        specs=[HBM] * 5,
        limit=60,
    )

    span = occupied * LANES
    source = jnp.arange(span, dtype=jnp.int32)[:, None]
    target = jnp.arange(span, dtype=jnp.int32)[None, :]
    spread = (target == source % LANES * occupied + source // LANES).astype(jnp.bfloat16)
    repeat = (
        jnp.arange(LANES, dtype=jnp.int32)[:, None] == jnp.arange(LANES * PAD, dtype=jnp.int32)[None, :] // PAD
    ).astype(jnp.bfloat16)
    earlier = jnp.arange(shells)[:, None] < jnp.arange(shells)[None, :]
    starts = jnp.sum(jnp.where(earlier[None], shell_len[:, :, None], 0), axis=1)
    starts = (starts + jnp.arange(count, dtype=jnp.int32)[:, None] * slab).reshape(-1)
    digits = jnp.stack([starts // DIGIT, starts % DIGIT, shell_len.reshape(-1)])
    shell_table = jnp.pad(digits, ((0, 5), (0, 0))).astype(jnp.bfloat16)

    half, parts = make_half(position, packed, vir_coeffs, spread, aux)
    state = {}

    def blocks_of(ks, halves):
        state["done"] = make_blocks(ks, count, capacity, state["meta"], halves, state["table"], state.get("done"))

    def first_blocks(halves):
        state["meta"], state["table"] = make_tables(
            position, parts, shell_table, repeat, pairs, capacity, shells, slab, width
        )
        blocks_of([0, 1, 2], halves)
        return state["done"][1]

    halves, sums = gather(half, count, "half", first_blocks)
    ks, _, held, out = state["done"]
    state["done"] = (ks, sums, held, out)
    blocks_of([3, *range(4, count, 2)], halves)
    for k in range(5, count, 2):
        blocks_of([k], halves)
    sums = state["done"][1]
    blocks = make_output(count, capacity, state["meta"], state["done"])
    sums = [sums] + [swap(sums, k, columns, "aux") for k in range(1, columns)]
    while len(sums) > 1:
        sums = [sums[n] + sums[n + 1] for n in range(0, len(sums), 2)]
    pair_scale = jnp.sqrt(sums[0].reshape(-1) / (NAUX * PAD * PAD) + 1e-06)
    return blocks, pair_scale


def solution(mesh):
    return jax.shard_map(
        per_device,
        mesh=mesh,
        in_specs=(
            P("aux", None, "rows"),
            P("rows", None),
            P(None, "rows"),
            P(),
            P("rows"),
            P("rows"),
            P("rows", None),
        ),
        out_specs=(P("rows", "aux", None), P("rows")),
        check_vma=False,
    )
```
